256 devices in a mesh: slab: 8 (over y, core), lat: 32 (over z, x).
Axes of the slice: x: 4, y: 4, z: 8, core: 2. Of those that a mesh axis runs over, the one named last changes fastest.
Arguments:
- weights: bfloat16 [3072, 16, 128, 128], P(('slab', 'lat')), may hold values from 0.0019989014 to 0.049804688
- angles: float32 [3072, 16, 3, 128], P(('slab', 'lat')), may hold values from 0.2 to 1
- block_list: int32 [3072, 16], P(('slab', 'lat')), may hold values from 0 to 16383, as said below
- observed: float32 [3072, 128], P(('slab', 'lat')), may hold values from -18 to 18
- ray_count: int32 [8, 32], P('slab', 'lat'), may hold values from 384 to 1536, as said below
Outputs:
- solution: float32 [64, 256, 3, 128], P('slab', 'lat')
- residual_ratio: float32 [], replicated
The draws below stay inside these ranges and needn't reach their ends.
Inputs may be any that keep to these rules, and one draw needn't show every extreme that they name: `block_list`: within the 192 entries of one device's ray tiles, at most 2 name blocks held by any one device (block z * 256 + x is held by slab z // 8, lat x // 8), and on every device some one holder is named exactly 2 times. Each device's live rays are the first ray_count of its rays in tile order; some device has all of them live.
All inputs are finite; a program needn't handle non-finite values.
Results may differ from the reference program's by a relative error of at most 0.004.
Values may be sent and summed in bfloat16 or wider, within the bound.
A program may use at most 64 MiB of HBM per device.

```python
import math
import jax
import jax.numpy as jnp
from jax import lax

RAYS_TILE = 128
BLOCK_CELLS = 128
TILE_BLOCKS = 16
TILES_DEV = 12
DEPTH_DEV = 8
CROSS_DEV = 8
ITERS = 3
DEPTH = 64
CROSS = 256
RAY_TILES = 3072
CAPACITY = 2
N_SLAB = 8
N_LAT = 32
DEVICES = 256


def draw_block_list(key, part):
    key = jax.random.fold_in(key, 7)
    device_total = N_SLAB * N_LAT
    entries = TILES_DEV * TILE_BLOCKS
    slot_total = device_total * CAPACITY
    owner_of_slot = jnp.arange(slot_total, dtype=jnp.int32) // CAPACITY
    within = jnp.arange(slot_total, dtype=jnp.int32) % CAPACITY

    def per_device(sub_key):
        key_rank, key_full, key_mix, key_inner = jax.random.split(sub_key, 4)
        ranks = jax.random.permutation(key_rank, slot_total).astype(jnp.int32)
        full_owner = jax.random.randint(key_full, (), 0, device_total)
        priority = jnp.where(owner_of_slot == full_owner, within - CAPACITY, ranks)
        chosen = jnp.argsort(priority)[:entries]
        holder = jax.random.permutation(key_mix, owner_of_slot[chosen])
        inner_block = jax.random.randint(key_inner, (entries,), 0, DEPTH_DEV * CROSS_DEV)
        own_slab = holder // N_LAT
        own_lat = holder % N_LAT
        depth_row = own_slab * DEPTH_DEV + inner_block // CROSS_DEV
        lateral = own_lat * CROSS_DEV + inner_block % CROSS_DEV
        return depth_row * CROSS + lateral
    all_lists = jax.vmap(per_device)(jax.random.split(key, device_total))
    return all_lists.reshape(RAY_TILES, TILE_BLOCKS).astype(jnp.int32)


def draw_ray_count(key, part):
    key = jax.random.fold_in(key, 13)
    key_count, key_busy = jax.random.split(key)
    device_total = N_SLAB * N_LAT
    ray_total = TILES_DEV * RAYS_TILE
    counts = jax.random.randint(key_count, (device_total,), ray_total // 4, ray_total + 1)
    busiest = jax.random.randint(key_busy, (), 0, device_total)
    counts = jnp.where(jnp.arange(device_total) == busiest, ray_total, counts)
    return counts.reshape(N_SLAB, N_LAT).astype(jnp.int32)


def block_scale(rng, extent, shards, smallest, top_value):
    gain, own = 1.0, jax.random.fold_in(rng, 6)
    for position, parts in shards:
        heights = jnp.exp(jax.random.uniform(jax.random.fold_in(own, position), (parts,), jnp.float32, smallest / len(shards), top_value / len(shards)))
        gain = gain * jnp.repeat(heights, extent[position] // parts).reshape([-1 if axis == position else 1 for axis in range(len(extent))])
    return gain


def centred(rng, shape, scale, bound, shards=(), held_as=jnp.bfloat16):
    level = block_scale(rng, shape, shards, -0.22, 0.18) if shards else 1.0
    values = jax.random.normal(rng, shape, jnp.float32) * scale * level
    return jnp.minimum(jnp.maximum(values, -bound), bound).astype(held_as)


def setup_inputs(seed: int = 0) -> dict:
    seeds = jax.random.split(jax.random.key(seed), 6)
    weights = jnp.clip(jnp.exp(math.log(0.049804688) - 3.2155114 * jax.random.uniform(seeds[0], (RAY_TILES, TILE_BLOCKS, RAYS_TILE, BLOCK_CELLS), jnp.float32) ** block_scale(seeds[0], (RAY_TILES, TILE_BLOCKS, RAYS_TILE, BLOCK_CELLS), ((0, 256),), -0.2, 0.2)), 0.0019989014, 0.049804688).astype(jnp.bfloat16)
    angles = jnp.clip(0.2 + 0.8 * jax.random.uniform(seeds[1], (RAY_TILES, TILE_BLOCKS, 3, RAYS_TILE), jnp.float32) ** block_scale(seeds[1], (RAY_TILES, TILE_BLOCKS, 3, RAYS_TILE), ((0, 256),), -0.2, 0.2), 0.2, 1.0)
    block_list = draw_block_list(jax.random.fold_in(seeds[5], 71), 0)
    observed = centred(seeds[3], (RAY_TILES, RAYS_TILE), 3.0, 18.0, ((0, 256),), jnp.float32)
    ray_count = draw_ray_count(jax.random.fold_in(seeds[5], 71), 0)
    return {"weights": weights, "angles": angles, "block_list": block_list, "observed": observed, "ray_count": ray_count}


smooth_weight = 0.3
tiny_eps = 1e-06

def laplace(field_values):
    padded = jnp.pad(field_values, ((1, 1), (1, 1), (0, 0), (1, 1)))
    centre = padded[1:-1, 1:-1, :, 1:-1]
    beside = padded[2:, 1:-1, :, 1:-1] + padded[:-2, 1:-1, :, 1:-1]
    beside = beside + padded[1:-1, 2:, :, 1:-1] + padded[1:-1, :-2, :, 1:-1]
    beside = beside + padded[1:-1, 1:-1, :, 2:] + padded[1:-1, 1:-1, :, :-2]
    return 6.0 * centre - beside

def grouped(array):
    return array.reshape((DEVICES, TILES_DEV) + array.shape[1:])

def forward_rays(weights, angles, block_list, model_vec):
    rounded = lax.optimization_barrier(model_vec.astype(jnp.bfloat16))
    blocks = rounded.reshape(DEPTH * CROSS, 3, BLOCK_CELLS)

    def per_group(operands):
        weight_part, angle_part, list_part = operands
        fetched = blocks[list_part].astype(jnp.float32)
        product = jnp.einsum('tkac,tkpc->tkpa', weight_part.astype(jnp.float32), fetched, precision=lax.Precision.HIGHEST)
        return lax.optimization_barrier(jnp.sum(product * angle_part, axis=(1, 2)))
    travel = lax.map(per_group, (grouped(weights), grouped(angles), grouped(block_list)))
    return travel.reshape(RAY_TILES, RAYS_TILE)

def adjoint_rays(weights, angles, block_list, ray_vec):

    def per_group(running, operands):
        weight_part, angle_part, list_part, ray_part = operands
        weighted = lax.optimization_barrier((angle_part * ray_part[:, None, None, :]).astype(jnp.bfloat16))
        product = jnp.einsum('tkac,tkpa->tkpc', weight_part.astype(jnp.float32), weighted.astype(jnp.float32), precision=lax.Precision.HIGHEST)
        running = running.at[list_part.reshape(-1)].add(product.reshape(-1, 3, BLOCK_CELLS))
        return (running, None)
    start = jnp.zeros((DEPTH * CROSS, 3, BLOCK_CELLS), jnp.float32)
    running, unused = lax.scan(per_group, start, (grouped(weights), grouped(angles), grouped(block_list), grouped(ray_vec)))
    return running.reshape(DEPTH, CROSS, 3, BLOCK_CELLS)

def reference(weights, angles, block_list, observed, ray_count):
    positions = jnp.arange(TILES_DEV)[:, None] * RAYS_TILE + jnp.arange(RAYS_TILE)[None, :]
    live_rays = (positions[None] < ray_count.reshape(DEVICES)[:, None, None]).astype(jnp.float32)
    live_rays = live_rays.reshape(RAY_TILES, RAYS_TILE)
    ray_vec = observed * live_rays
    first_norm = jnp.sqrt(jnp.sum(ray_vec * ray_vec) + tiny_eps)
    ray_vec = ray_vec / first_norm
    model_vec = adjoint_rays(weights, angles, block_list, ray_vec)
    v_norm = jnp.sqrt(jnp.sum(model_vec * model_vec) + tiny_eps)
    model_vec = model_vec / v_norm
    direction = model_vec
    solution = jnp.zeros_like(model_vec)
    cell_vec = jnp.zeros_like(model_vec)
    phi_bar = first_norm
    rho_bar = v_norm
    for iteration in range(ITERS):
        ray_vec = forward_rays(weights, angles, block_list, model_vec) * live_rays - v_norm * ray_vec
        cell_vec = smooth_weight * laplace(model_vec) - v_norm * cell_vec
        u_norm = jnp.sqrt(jnp.sum(ray_vec * ray_vec) + jnp.sum(cell_vec * cell_vec) + tiny_eps)
        ray_vec = ray_vec / u_norm
        cell_vec = cell_vec / u_norm
        model_vec = adjoint_rays(weights, angles, block_list, ray_vec) + smooth_weight * laplace(cell_vec) - u_norm * model_vec
        v_norm = jnp.sqrt(jnp.sum(model_vec * model_vec) + tiny_eps)
        model_vec = model_vec / v_norm
        rho_now = jnp.sqrt(rho_bar * rho_bar + u_norm * u_norm)
        cos_term = rho_bar / rho_now
        sin_term = u_norm / rho_now
        theta_now = sin_term * v_norm
        rho_bar = -cos_term * v_norm
        phi_now = cos_term * phi_bar
        phi_bar = sin_term * phi_bar
        solution = solution + phi_now / rho_now * direction
        direction = model_vec - theta_now / rho_now * direction
    return (solution, phi_bar / first_norm)
```

```python
import functools

import jax
import jax.numpy as jnp
from jax import lax
from jax.experimental import pallas as pl
from jax.experimental.pallas import tpu as pltpu
from jax.sharding import PartitionSpec as P

MESH = pl.DeviceIdType.MESH
F32 = jnp.float32
BF16 = jnp.bfloat16

TILES = 12
BLOCKS = 16
ENTRIES = TILES * BLOCKS
DEVICES = 256
N_SLAB = 8
N_LAT = 32
SLOTS = 2 * DEVICES
LOCAL = 64
ROW = 384
ITERS = 3
GROUPS = 4
GROUP = DEVICES // GROUPS
EXCHANGES = 2 * ITERS
HALOS = EXCHANGES - 1
SUMS = EXCHANGES + 1
LAM = 0.3
EPS = 1e-6


def dot(a, b):
    return lax.dot_general(a, b, (((1,), (0,)), ((), ())), preferred_element_type=F32)


def iota(shape, dim):
    return lax.broadcasted_iota(jnp.int32, shape, dim).astype(F32)


def one_hot(same):
    return jnp.where(same, 1.0, 0.0).astype(BF16)


def wait_bytes(ref, sem):
    pltpu.make_async_copy(ref, ref, sem).wait()


def block_diagonal(rows):
    place = lax.broadcasted_iota(jnp.int32, rows.shape, 0) % BLOCKS
    empty = jnp.zeros_like(rows)
    return jnp.concatenate([jnp.where(place == k, rows, empty) for k in range(BLOCKS)], axis=1)


def kernel(
    w_hbm, ang_ref, ids_ref, obs_ref, cnt_ref, out_ref, ratio_ref,
    W, WT, S, ST, STL, PICK, PICKT, RAY, TRAV, PART, FETCH, LIVE,
    X0, R0, X, R, V, FACE, HALO, AX, AY, AZ,
    wsem, xsend, xrecv, hsend, hrecv, s1, r1, s2, r2, entered,
):
    s, l = lax.axis_index("slab"), lax.axis_index("lat")
    me = s * N_LAT + l
    y, c, z, x = lax.div(s, 2), lax.rem(s, 2), lax.div(l, 4), lax.rem(l, 4)
    a_me, b_me = z * 2 + c, y * 4 + x

    def a_dev(j):
        return (y * 2 + lax.rem(j, 2), lax.div(j, 2) * 4 + x)

    def b_dev(j):
        return (lax.div(j, 4) * 2 + c, z * 4 + lax.rem(j, 4))

    for t in range(TILES):
        pltpu.make_async_copy(w_hbm.at[t], W.at[t], wsem.at[t]).start()

    barrier = pltpu.get_barrier_semaphore()

    @pl.loop(1, 16)
    def _(j):
        pl.semaphore_signal(barrier, inc=1, device_id=a_dev(lax.rem(a_me + j, 16)), device_id_type=MESH)
        pl.semaphore_signal(barrier, inc=1, device_id=b_dev(lax.rem(b_me + j, 16)), device_id_type=MESH)

    ids = ids_ref[...]
    depth, cross = ids >> 8, ids & 255
    owner = ((depth >> 3) * N_LAT + (cross >> 3) - me) & 255
    inner = (depth & 7) * 8 + (cross & 7)
    owner_r, inner_r = owner.astype(F32), inner.astype(F32)
    square = (ENTRIES, ENTRIES)
    i0, i1 = iota(square, 0), iota(square, 1)

    def column(row):
        return jnp.sum(jnp.where(i0 == i1, row, 0.0), axis=1, keepdims=True)

    owner_c, inner_c = column(owner_r), column(inner_r)
    same = jnp.where(owner_r == owner_c, 1.0, 0.0)
    slot_c = 2.0 * owner_c + jnp.sum(jnp.where(i1 < i0, same, 0.0), axis=1, keepdims=True)
    slot_r = 2.0 * owner_r + jnp.sum(jnp.where(i0 < i1, same, 0.0), axis=0, keepdims=True)
    alone = jnp.sum(same, axis=0, keepdims=True) == 1.0
    spare_r = jnp.where(alone, slot_r + 1.0, -1.0)
    S[...] = one_hot(iota((ENTRIES, SLOTS), 1) == slot_c)
    st = one_hot(iota((SLOTS, ENTRIES), 0) == slot_r)
    stl = one_hot(iota((SLOTS, ENTRIES), 0) == spare_r)
    ST[...] = st
    STL[...] = stl
    wanted = dot(st + stl, one_hot(iota((ENTRIES, 128), 1) == inner_c)).astype(BF16)

    at = iota((TILES, 128), 0) * 128.0 + iota((TILES, 128), 1)
    LIVE[...] = jnp.where(at < cnt_ref[0, 0].astype(F32), 1.0, 0.0)

    def total_row(values):
        return jnp.sum(values, axis=0, keepdims=True)

    def sum_first(n, row):
        AX[n, 0] = row
        AY[n, a_me] = row

        @pl.loop(1, 16)
        def _(j):
            pltpu.make_async_remote_copy(
                AX.at[n, 0], AY.at[n, a_me], s1.at[n], r1.at[n],
                device_id=a_dev(lax.rem(a_me + j, 16)), device_id_type=MESH,
            ).start()

    def sum_second(n):
        wait_bytes(AY.at[n, pl.ds(0, 15)], r1.at[n])
        row = jnp.sum(AY[n], axis=0)
        AX[n, 1] = row
        AZ[n, b_me] = row

        @pl.loop(1, 16)
        def _(j):
            pltpu.make_async_remote_copy(
                AX.at[n, 1], AZ.at[n, b_me], s2.at[n], r2.at[n],
                device_id=b_dev(lax.rem(b_me + j, 16)), device_id_type=MESH,
            ).start()

    def sum_third(n):
        wait_bytes(AZ.at[n, pl.ds(0, 15)], r2.at[n])
        total = jnp.sum(jnp.sum(AZ[n], axis=0), axis=1, keepdims=True)
        return jnp.sqrt(jnp.broadcast_to(total, (1, 128)) + EPS)

    def buffers(e):
        return (X0, R0) if e == 0 else (X.at[e - 1], R.at[e - 1])

    def send_group(e, g, forward):
        src, dst = buffers(e)

        def send(j):
            d = lax.rem(me + j if forward else me + DEVICES - j, DEVICES)
            pltpu.make_async_remote_copy(
                src.at[j], dst.at[j], xsend.at[e], xrecv.at[e, g],
                device_id=(lax.div(d, N_LAT), lax.rem(d, N_LAT)), device_id_type=MESH,
            ).start()

        if g == 0:
            pltpu.make_async_copy(src.at[0], dst.at[0], xrecv.at[e, 0]).start()

        @pl.loop(max(g * GROUP, 1), (g + 1) * GROUP)
        def _(j):
            send(j)

    def receive_group(e, g):
        dst = buffers(e)[1].at[pl.ds(g * GROUP, GROUP)]
        wait_bytes(dst, xrecv.at[e, g])
        return dst[...].reshape(2 * GROUP, dst.shape[-1])

    def send_halo(h):
        for p in range(3):
            v = V[h, p]
            FACE[h, 0, p] = jnp.concatenate([v[8 * i:8 * i + 1] for i in range(8)], axis=0)
            FACE[h, 1, p] = jnp.concatenate([v[8 * i + 7:8 * i + 8] for i in range(8)], axis=0)
        before, after = lax.rem(s + N_SLAB - 1, N_SLAB), lax.rem(s + 1, N_SLAB)
        left, right = lax.rem(l + N_LAT - 1, N_LAT), lax.rem(l + 1, N_LAT)
        moves = (
            (V.at[h, :, pl.ds(56, 8)], 0, (after, l)),
            (V.at[h, :, pl.ds(0, 8)], 1, (before, l)),
            (FACE.at[h, 1], 2, (s, right)),
            (FACE.at[h, 0], 3, (s, left)),
        )
        for src, side, device in moves:
            pltpu.make_async_remote_copy(
                src, HALO.at[h, side], hsend.at[h, side], hrecv.at[h, side],
                device_id=device, device_id_type=MESH,
            ).start()

    def laplace(h):
        for side in range(4):
            wait_bytes(HALO.at[h, side], hrecv.at[h, side])
        row = lax.broadcasted_iota(jnp.int32, (LOCAL, 128), 0) % 8
        lane = lax.broadcasted_iota(jnp.int32, (LOCAL, 128), 1)

        def spread(face):
            return jnp.concatenate([jnp.broadcast_to(face[i:i + 1], (8, 128)) for i in range(8)], axis=0)

        result = []
        for p in range(3):
            v = V[h, p]
            low = jnp.where(s > 0, HALO[h, 0, p], 0.0)
            high = jnp.where(s < N_SLAB - 1, HALO[h, 1, p], 0.0)
            left = jnp.where(l > 0, HALO[h, 2, p], 0.0)
            right = jnp.where(l < N_LAT - 1, HALO[h, 3, p], 0.0)
            beside = jnp.concatenate([low, v[:56]], axis=0) + jnp.concatenate([v[8:], high], axis=0)
            beside = beside + jnp.where(row == 0, spread(left), pltpu.roll(v, 1, 0))
            beside = beside + jnp.where(row == 7, spread(right), pltpu.roll(v, LOCAL - 1, 0))
            beside = beside + jnp.where(lane == 0, 0.0, pltpu.roll(v, 1, 1))
            beside = beside + jnp.where(lane == 127, 0.0, pltpu.roll(v, 127, 1))
            result.append(6.0 * v - beside)
        return result

    def adjoint(first):
        def tile(t, carry):
            if first:
                wait_bytes(W.at[t], wsem.at[t])
            weighted = ang_ref[t] * RAY[pl.ds(t, 1), :]
            high = weighted.astype(BF16)
            low = (weighted - high.astype(F32)).astype(BF16)
            rows = block_diagonal(jnp.concatenate([high, low], axis=0))
            out = dot(rows, W[t].reshape(BLOCKS * 128, 128))
            out = out[:48] + out[48:]
            for p in range(3):
                PART[p, pl.ds(pl.multiple_of(t * BLOCKS, BLOCKS), BLOCKS), :] = out[p * BLOCKS:(p + 1) * BLOCKS]
            return carry

        lax.fori_loop(0, TILES, tile, 0, unroll=2)

    def send_adjoint(e):
        high = [PART[p].astype(BF16) for p in range(3)]
        low = [(PART[p] - high[p].astype(F32)).astype(BF16) for p in range(3)]
        high, low = jnp.concatenate(high, axis=1), jnp.concatenate(low, axis=1)
        for g in range(GROUPS):
            at = pl.ds(g * 2 * GROUP, 2 * GROUP)
            rows = (dot(ST[at, :], high) + dot(STL[at, :], low)).astype(BF16)
            if e == 0:
                rows = jnp.concatenate([rows, wanted[g * 2 * GROUP:(g + 1) * 2 * GROUP]], axis=1)
            src = buffers(e)[0]
            src[pl.ds(g * GROUP, GROUP)] = rows.reshape(GROUP, 2, rows.shape[-1])
            if g == GROUPS - 1:
                sum_second(e)
            send_group(e, g, True)

    def send_forward(e, model):
        model = jnp.concatenate(model, axis=1).astype(BF16)
        for g in range(GROUPS):
            rows = dot(PICK[pl.ds(g * 2 * GROUP, 2 * GROUP), :], model).astype(BF16)
            buffers(e)[0][pl.ds(g * GROUP, GROUP)] = rows.reshape(GROUP, 2, ROW)
            if g == GROUPS - 1:
                sum_second(e)
            send_group(e, g, False)

    def collect(e):
        total = None
        for g in range(GROUPS):
            rows = receive_group(e, g)
            part = dot(PICKT[g], rows)
            total = part if total is None else total + part
        return [total[:, p * 128:(p + 1) * 128] for p in range(3)]

    def travel(e):
        total = None
        for g in range(GROUPS):
            rows = receive_group(e, g)
            part = dot(S[:, pl.ds(g * 2 * GROUP, 2 * GROUP)], rows)
            total = part if total is None else total + part
        FETCH[...] = total.astype(BF16)

        def tile(t, carry):
            at = pl.ds(pl.multiple_of(t * BLOCKS, BLOCKS), BLOCKS)
            rows = jnp.concatenate([FETCH[at, p * 128:(p + 1) * 128] for p in range(3)], axis=0)
            out = dot(block_diagonal(rows), WT[t]) * ang_ref[t]
            TRAV[pl.ds(t, 1), :] = jnp.sum(out, axis=0, keepdims=True)
            return carry

        lax.fori_loop(0, TILES, tile, 0, unroll=2)
        return TRAV[...]

    ray = obs_ref[...] * LIVE[...]
    RAY[...] = ray
    adjoint(True)
    pl.semaphore_wait(barrier, 30)

    @pl.loop(1, 16)
    def _(j):
        pl.semaphore_signal(entered, inc=1, device_id=b_dev(lax.rem(b_me + j, 16)), device_id_type=MESH)

    pl.semaphore_wait(entered, 15)
    sum_first(0, total_row(ray * ray))
    send_adjoint(0)

    def turn(t, carry):
        for k in range(BLOCKS):
            WT[t, k * 128:(k + 1) * 128, :] = W[t, k].T
        return carry

    lax.fori_loop(0, TILES, turn, 0)
    norm = sum_third(0)
    first_norm = norm
    ray = ray / norm
    total = None
    for g in range(GROUPS):
        rows = receive_group(0, g)
        pick = rows[:, ROW:ROW + LOCAL]
        PICK[pl.ds(g * 2 * GROUP, 2 * GROUP), :] = pick
        PICKT[g] = pick.T
        part = dot(PICKT[g], rows[:, :ROW])
        total = part if total is None else total + part
    model_raw = [total[:, p * 128:(p + 1) * 128] / norm for p in range(3)]

    cell = [jnp.zeros((LOCAL, 128), F32) for _ in range(3)]
    direction = None
    phi_bar = first_norm
    rho_bar = u_norm = rho_now = sin_term = cos_term = None
    result = [jnp.zeros((LOCAL, 128), F32) for _ in range(3)]
    for i in range(ITERS):
        e = 2 * i + 1
        for p in range(3):
            V[e - 1, p] = model_raw[p]
        sum_first(e, total_row(sum(v * v for v in model_raw)))
        send_halo(e - 1)
        send_forward(e, model_raw)
        smooth = laplace(e - 1)
        v_norm = sum_third(e)
        model = [v / v_norm for v in model_raw]
        if i == 0:
            rho_bar = v_norm
            direction = model
        else:
            theta = sin_term * v_norm
            rho_bar = -cos_term * v_norm
            direction = [m - theta / rho_now * d for m, d in zip(model, direction)]
        cell_raw = [LAM * sm / v_norm - v_norm * q for sm, q in zip(smooth, cell)]
        cell_sum = total_row(sum(q * q for q in cell_raw))
        if i < ITERS - 1:
            for p in range(3):
                V[e, p] = cell_raw[p]
        ray_raw = travel(e) * LIVE[...] / v_norm - v_norm * ray
        sum_first(e + 1, cell_sum + total_row(ray_raw * ray_raw))
        if i < ITERS - 1:
            send_halo(e)
            RAY[...] = ray_raw
            adjoint(False)
            send_adjoint(e + 1)
            smooth = laplace(e)
        else:
            sum_second(e + 1)
        u_norm = sum_third(e + 1)
        rho_now = jnp.sqrt(rho_bar * rho_bar + u_norm * u_norm)
        cos_term = rho_bar / rho_now
        sin_term = u_norm / rho_now
        phi_now = cos_term * phi_bar
        phi_bar = sin_term * phi_bar
        result = [r + phi_now / rho_now * d for r, d in zip(result, direction)]
        if i < ITERS - 1:
            ray = ray_raw / u_norm
            cell = [q / u_norm for q in cell_raw]
            back = collect(e + 1)
            model_raw = [
                b / u_norm + LAM * sm / u_norm - u_norm * m for b, sm, m in zip(back, smooth, model)
            ]

    for p in range(3):
        out_ref[p] = result[p]
    ratio_ref[...] = phi_bar / first_norm

    for e in range(EXCHANGES):
        wait_bytes(buffers(e)[0].at[pl.ds(0, DEVICES - 1)], xsend.at[e])
    for h in range(HALOS):
        for side in range(4):
            wait_bytes(HALO.at[h, side], hsend.at[h, side])
    for n in range(SUMS):
        wait_bytes(AY.at[n, pl.ds(0, 15)], s1.at[n])
        wait_bytes(AZ.at[n, pl.ds(0, 15)], s2.at[n])


def shards(weights, angles, block_list, observed, ray_count):
    ids = block_list.reshape(1, ENTRIES)
    ang = angles.transpose(0, 2, 1, 3).reshape(TILES, 3 * BLOCKS, 128)
    vmem = pl.BlockSpec(memory_space=pltpu.VMEM)
    dma = pltpu.SemaphoreType.DMA
    out, ratio = pl.pallas_call(
        kernel,
        out_shape=(
            jax.ShapeDtypeStruct((3, LOCAL, 128), F32),
            jax.ShapeDtypeStruct((1, 128), F32),
        ),
        in_specs=[pl.BlockSpec(memory_space=pl.ANY), vmem, vmem, vmem, pl.BlockSpec(memory_space=pltpu.SMEM)],
        out_specs=(vmem, vmem),
        scratch_shapes=[
            pltpu.VMEM((TILES, BLOCKS, 128, 128), BF16),
            pltpu.VMEM((TILES, BLOCKS * 128, 128), BF16),
            pltpu.VMEM((ENTRIES, SLOTS), BF16),
            pltpu.VMEM((SLOTS, ENTRIES), BF16),
            pltpu.VMEM((SLOTS, ENTRIES), BF16),
            pltpu.VMEM((SLOTS, LOCAL), BF16),
            pltpu.VMEM((GROUPS, LOCAL, 2 * GROUP), BF16),
            pltpu.VMEM((TILES, 128), F32),
            pltpu.VMEM((TILES, 128), F32),
            pltpu.VMEM((3, ENTRIES, 128), F32),
            pltpu.VMEM((ENTRIES, ROW), BF16),
            pltpu.VMEM((TILES, 128), F32),
            pltpu.VMEM((DEVICES, 2, ROW + 128), BF16),
            pltpu.VMEM((DEVICES, 2, ROW + 128), BF16),
            pltpu.VMEM((EXCHANGES - 1, DEVICES, 2, ROW), BF16),
            pltpu.VMEM((EXCHANGES - 1, DEVICES, 2, ROW), BF16),
            pltpu.VMEM((HALOS, 3, LOCAL, 128), F32),
            pltpu.VMEM((HALOS, 2, 3, 8, 128), F32),
            pltpu.VMEM((HALOS, 4, 3, 8, 128), F32),
            pltpu.VMEM((SUMS, 2, 1, 128), F32),
            pltpu.VMEM((SUMS, 16, 1, 128), F32),
            pltpu.VMEM((SUMS, 16, 1, 128), F32),
            dma((TILES,)),
            dma((EXCHANGES,)),
            dma((EXCHANGES, GROUPS)),
            dma((HALOS, 4)),
            dma((HALOS, 4)),
            dma((SUMS,)),
            dma((SUMS,)),
            dma((SUMS,)),
            dma((SUMS,)),
            pltpu.SemaphoreType.REGULAR,
        ],
        compiler_params=pltpu.CompilerParams(
            collective_id=0, has_side_effects=True, vmem_limit_bytes=56 * 1024 * 1024
        ),
    )(weights, ang, ids, observed, ray_count)
    out = out.reshape(3, 8, 8, 128).transpose(1, 2, 0, 3)
    return out, ratio[0, 0]


def solution(mesh):
    placed = (
        P(("slab", "lat"), None, None, None),
        P(("slab", "lat"), None, None, None),
        P(("slab", "lat"), None),
        P(("slab", "lat"), None),
        P("slab", "lat"),
    )
    return jax.shard_map(
        shards,
        mesh=mesh,
        in_specs=placed,
        out_specs=(P("slab", "lat", None, None), P()),
        check_vma=False,
    )
```

```python
import functools

import jax
import jax.numpy as jnp
from jax import lax
from jax.experimental import pallas as pl
from jax.experimental.pallas import tpu as pltpu
from jax.sharding import PartitionSpec as P

MESH = pl.DeviceIdType.MESH
F32 = jnp.float32
BF16 = jnp.bfloat16

TILES = 12
BLOCKS = 16
ENTRIES = TILES * BLOCKS
DEVICES = 256
N_SLAB = 8
N_LAT = 32
SLOTS = 2 * DEVICES
LOCAL = 64
ROW = 384
ITERS = 3
GROUPS = 8
FAR = (4, 5, 3, 6)
NEAR = (2, 7, 1, 0)
GROUP = DEVICES // GROUPS
EXCHANGES = 2 * ITERS
HALOS = EXCHANGES - 1
SUMS = EXCHANGES + 1
LAM = 0.3
EPS = 1e-6


def dot(a, b):
    return lax.dot_general(a, b, (((1,), (0,)), ((), ())), preferred_element_type=F32)


def iota(shape, dim):
    return lax.broadcasted_iota(jnp.int32, shape, dim).astype(F32)


def one_hot(same):
    return jnp.where(same, 1.0, 0.0).astype(BF16)


def wait_bytes(ref, sem):
    pltpu.make_async_copy(ref, ref, sem).wait()


def block_diagonal(rows):
    place = lax.broadcasted_iota(jnp.int32, rows.shape, 0) % BLOCKS
    empty = jnp.zeros_like(rows)
    return jnp.concatenate([jnp.where(place == k, rows, empty) for k in range(BLOCKS)], axis=1)


def kernel(
    w_hbm, ang_ref, ids_ref, obs_ref, cnt_ref, out_ref, ratio_ref,
    W, WT, S, ST, STL, PICK, PICKT, RAY, PART, FETCH, LIVE,
    X0, R0, X, R, V, FACE, HALO, AX, AY, AZ,
    wsem, xsend, xrecv, hsend, hrecv, s1, r1, s2, r2, entered,
):
    s, l = lax.axis_index("slab"), lax.axis_index("lat")
    me = s * N_LAT + l
    y, c, z, x = lax.div(s, 2), lax.rem(s, 2), lax.div(l, 4), lax.rem(l, 4)
    a_me, b_me = z * 2 + c, y * 4 + x

    def a_dev(j):
        return (y * 2 + lax.rem(j, 2), lax.div(j, 2) * 4 + x)

    def b_dev(j):
        return (lax.div(j, 4) * 2 + c, z * 4 + lax.rem(j, 4))

    for t in range(TILES):
        pltpu.make_async_copy(w_hbm.at[t], W.at[t], wsem.at[t]).start()

    barrier = pltpu.get_barrier_semaphore()

    @pl.loop(1, 16)
    def _(j):
        pl.semaphore_signal(barrier, inc=1, device_id=a_dev(lax.rem(a_me + j, 16)), device_id_type=MESH)
        pl.semaphore_signal(barrier, inc=1, device_id=b_dev(lax.rem(b_me + j, 16)), device_id_type=MESH)

    spread_k = jnp.where(
        (lax.broadcasted_iota(jnp.int32, (BLOCKS, ENTRIES), 1) & (BLOCKS - 1))
        == lax.broadcasted_iota(jnp.int32, (BLOCKS, ENTRIES), 0),
        1.0, 0.0,
    ).astype(BF16)
    own_tile = (lax.broadcasted_iota(jnp.int32, (TILES, ENTRIES), 1) >> 4) == lax.broadcasted_iota(
        jnp.int32, (TILES, ENTRIES), 0
    )

    def in_a_row(values):
        spread = dot(values.astype(F32).astype(BF16), spread_k)
        return jnp.sum(jnp.where(own_tile, spread, 0.0), axis=0, keepdims=True).astype(jnp.int32)

    ids = ids_ref[...]
    depth, cross = in_a_row(ids >> 8), in_a_row(ids & 255)
    inner = (depth & 7) * 8 + (cross & 7)
    slab_o, lat_o = depth >> 3, cross >> 3
    dx, dz = ((lat_o & 3) - x) & 3, ((lat_o >> 2) - z) & 7
    dy, dc = ((slab_o >> 1) - y) & 3, ((slab_o & 1) - c) & 1

    def far_first(d):
        return jnp.where(d == 0, 3, jnp.where(d == 1, 2, jnp.where(d == 2, 0, 1)))

    place_z = jnp.zeros_like(dz)
    for k in range(4):
        place_z = jnp.where(dz == FAR[k], k, place_z)
        place_z = jnp.where(dz == NEAR[k], 128 + k, place_z)
    owner = place_z + 4 * ((far_first(dx) * 4 + far_first(dy)) * 2 + 1 - dc)
    owner_r, inner_r = owner.astype(F32), inner.astype(F32)
    square = (ENTRIES, ENTRIES)
    i0, i1 = iota(square, 0), iota(square, 1)

    def column(row):
        return jnp.sum(jnp.where(i0 == i1, row, 0.0), axis=1, keepdims=True)

    owner_c, inner_c = column(owner_r), column(inner_r)
    same = jnp.where(owner_r == owner_c, 1.0, 0.0)
    slot_c = 2.0 * owner_c + jnp.sum(jnp.where(i1 < i0, same, 0.0), axis=1, keepdims=True)
    slot_r = 2.0 * owner_r + jnp.sum(jnp.where(i0 < i1, same, 0.0), axis=0, keepdims=True)
    alone = jnp.sum(same, axis=0, keepdims=True) == 1.0
    spare_r = jnp.where(alone, slot_r + 1.0, -1.0)
    for g in range(GROUPS):
        S[g] = one_hot(iota((ENTRIES, 2 * GROUP), 1) + float(2 * GROUP * g) == slot_c)
    st = one_hot(iota((SLOTS, ENTRIES), 0) == slot_r)
    stl = one_hot(iota((SLOTS, ENTRIES), 0) == spare_r)
    ST[...] = st
    STL[...] = stl
    wanted = dot(st + stl, one_hot(iota((ENTRIES, 128), 1) == inner_c)).astype(BF16)

    at = iota((TILES, 128), 0) * 128.0 + iota((TILES, 128), 1)
    LIVE[...] = jnp.where(at < cnt_ref[0, 0].astype(F32), 1.0, 0.0)

    def total_row(values):
        return jnp.sum(values, axis=0, keepdims=True)

    def sum_first(n, row):
        AX[n, 0] = row
        AY[n, a_me] = row

        @pl.loop(1, 16)
        def _(j):
            pltpu.make_async_remote_copy(
                AX.at[n, 0], AY.at[n, a_me], s1.at[n], r1.at[n],
                device_id=a_dev(lax.rem(a_me + j, 16)), device_id_type=MESH,
            ).start()

    def sum_second(n):
        wait_bytes(AY.at[n, pl.ds(0, 15)], r1.at[n])
        row = jnp.sum(AY[n], axis=0)
        AX[n, 1] = row
        AZ[n, b_me] = row

        @pl.loop(1, 16)
        def _(j):
            pltpu.make_async_remote_copy(
                AX.at[n, 1], AZ.at[n, b_me], s2.at[n], r2.at[n],
                device_id=b_dev(lax.rem(b_me + j, 16)), device_id_type=MESH,
            ).start()

    def sum_third(n):
        wait_bytes(AZ.at[n, pl.ds(0, 15)], r2.at[n])
        total = jnp.sum(jnp.sum(AZ[n], axis=0), axis=1, keepdims=True)
        return jnp.sqrt(jnp.broadcast_to(total, (1, 128)) + EPS)

    def buffers(e):
        return (X0, R0) if e == 0 else (X.at[e - 1], R.at[e - 1])

    def send_group(e, g, forward):
        src, dst = buffers(e)
        steps = FAR if g < GROUPS // 2 else NEAR

        def offset(i):
            far = 3 - i
            return lax.rem(lax.div(far * (far + 1), 2), 4)

        def place(at, d, n):
            return lax.rem(at + n - d, n) if forward else lax.rem(at + d, n)

        def one(q, k, to_x, to_slab):
            j = (g // (GROUPS // 2)) * 128 + q * 4 + k
            to_z = lax.rem(z + (8 - steps[k] if forward else steps[k]), 8)
            pltpu.make_async_remote_copy(
                src.at[j], dst.at[j], xsend.at[e], xrecv.at[e, g],
                device_id=(to_slab, to_z * 4 + to_x), device_id_type=MESH,
            ).start()

        first = (g % (GROUPS // 2)) * (GROUP // 4)
        last = first + GROUP // 4

        @pl.loop(first, last - 1 if g == GROUPS - 1 else last)
        def _(q):
            to_x = place(x, offset(lax.div(q, 8)), 4)
            to_y = place(y, offset(lax.rem(lax.div(q, 2), 4)), 4)
            to_c = lax.rem(c + 1 - lax.rem(q, 2), 2)
            for k in range(4):
                one(q, k, to_x, to_y * 2 + to_c)

        if g == GROUPS - 1:
            for k in range(3):
                one(31, k, x, s)
            pltpu.make_async_copy(src.at[DEVICES - 1], dst.at[DEVICES - 1], xrecv.at[e, g]).start()

    def receive_group(e, g):
        dst = buffers(e)[1].at[pl.ds(g * GROUP, GROUP)]
        wait_bytes(dst, xrecv.at[e, g])
        return dst[...].reshape(2 * GROUP, dst.shape[-1])

    def send_halo(h):
        for p in range(3):
            v = V[h, p]
            FACE[h, 0, p] = jnp.concatenate([v[8 * i:8 * i + 1] for i in range(8)], axis=0)
            FACE[h, 1, p] = jnp.concatenate([v[8 * i + 7:8 * i + 8] for i in range(8)], axis=0)
        before, after = lax.rem(s + N_SLAB - 1, N_SLAB), lax.rem(s + 1, N_SLAB)
        left, right = lax.rem(l + N_LAT - 1, N_LAT), lax.rem(l + 1, N_LAT)
        moves = (
            (V.at[h, :, pl.ds(56, 8)], 0, (after, l)),
            (V.at[h, :, pl.ds(0, 8)], 1, (before, l)),
            (FACE.at[h, 1], 2, (s, right)),
            (FACE.at[h, 0], 3, (s, left)),
        )
        for src, side, device in moves:
            pltpu.make_async_remote_copy(
                src, HALO.at[h, side], hsend.at[h, side], hrecv.at[h, side],
                device_id=device, device_id_type=MESH,
            ).start()

    def laplace(h):
        for side in range(4):
            wait_bytes(HALO.at[h, side], hrecv.at[h, side])
        row = lax.broadcasted_iota(jnp.int32, (LOCAL, 128), 0) % 8
        lane = lax.broadcasted_iota(jnp.int32, (LOCAL, 128), 1)

        def spread(face):
            return jnp.concatenate([jnp.broadcast_to(face[i:i + 1], (8, 128)) for i in range(8)], axis=0)

        result = []
        for p in range(3):
            v = V[h, p]
            low = jnp.where(s > 0, HALO[h, 0, p], 0.0)
            high = jnp.where(s < N_SLAB - 1, HALO[h, 1, p], 0.0)
            left = jnp.where(l > 0, HALO[h, 2, p], 0.0)
            right = jnp.where(l < N_LAT - 1, HALO[h, 3, p], 0.0)
            beside = jnp.concatenate([low, v[:56]], axis=0) + jnp.concatenate([v[8:], high], axis=0)
            beside = beside + jnp.where(row == 0, spread(left), pltpu.roll(v, 1, 0))
            beside = beside + jnp.where(row == 7, spread(right), pltpu.roll(v, LOCAL - 1, 0))
            beside = beside + jnp.where(lane == 0, 0.0, pltpu.roll(v, 1, 1))
            beside = beside + jnp.where(lane == 127, 0.0, pltpu.roll(v, 127, 1))
            result.append(6.0 * v - beside)
        return result

    def forward_tile(t):
        rows = jnp.concatenate(
            [FETCH[t * BLOCKS:(t + 1) * BLOCKS, p * 128:(p + 1) * 128] for p in range(3)], axis=0
        )
        return total_row(dot(block_diagonal(rows), WT[t]) * ang_ref[t])

    def adjoint_tile(t, ray_row):
        weighted = ang_ref[t] * ray_row
        high = weighted.astype(BF16)
        low = (weighted - high.astype(F32)).astype(BF16)
        rows = block_diagonal(jnp.concatenate([high, low], axis=0))
        out = dot(rows, W[t].reshape(BLOCKS * 128, 128))
        out = out[:48] + out[48:]
        for p in range(3):
            PART[p, t * BLOCKS:(t + 1) * BLOCKS, :] = out[p * BLOCKS:(p + 1) * BLOCKS]

    def send_adjoint(e, after_first):
        high = [PART[p].astype(BF16) for p in range(3)]
        low = [(PART[p] - high[p].astype(F32)).astype(BF16) for p in range(3)]
        high, low = jnp.concatenate(high, axis=1), jnp.concatenate(low, axis=1)
        for g in range(GROUPS):
            at = pl.ds(g * 2 * GROUP, 2 * GROUP)
            rows = (dot(ST[at, :], high) + dot(STL[at, :], low)).astype(BF16)
            if e == 0:
                rows = jnp.concatenate([rows, wanted[g * 2 * GROUP:(g + 1) * 2 * GROUP]], axis=1)
            src = buffers(e)[0]
            src[pl.ds(g * GROUP, GROUP)] = rows.reshape(GROUP, 2, rows.shape[-1])
            send_group(e, g, False)
            if g == 0:
                after_first()
        sum_second(e)

    def send_forward(e, model, after_first):
        model = jnp.concatenate(model, axis=1).astype(BF16)
        for g in range(GROUPS):
            rows = dot(PICK[pl.ds(g * 2 * GROUP, 2 * GROUP), :], model).astype(BF16)
            buffers(e)[0][pl.ds(g * GROUP, GROUP)] = rows.reshape(GROUP, 2, ROW)
            send_group(e, g, True)
            if g == 0:
                after_first()
        sum_second(e)

    def gather(e, table, groups, total=None):
        for g in groups:
            part = dot(table[g], receive_group(e, g))
            total = part if total is None else total + part
        return total

    def by_parameter(total):
        return [total[:, p * 128:(p + 1) * 128] for p in range(3)]

    ray = obs_ref[...] * LIVE[...]
    RAY[...] = ray
    pl.semaphore_wait(barrier, 30)

    @pl.loop(1, 16)
    def _(j):
        pl.semaphore_signal(entered, inc=1, device_id=b_dev(lax.rem(b_me + j, 16)), device_id_type=MESH)

    for t in range(TILES):
        wait_bytes(W.at[t], wsem.at[t])
        adjoint_tile(t, RAY[t:t + 1, :])
    pl.semaphore_wait(entered, 15)
    send_adjoint(0, lambda: sum_first(0, total_row(ray * ray)))

    def turn(t, carry):
        for k in range(BLOCKS):
            WT[t, k * 128:(k + 1) * 128, :] = W[t, k].T
        return carry

    lax.fori_loop(0, TILES, turn, 0)
    total = None
    for g in range(GROUPS):
        rows = receive_group(0, g)
        pick = rows[:, ROW:ROW + LOCAL]
        PICK[pl.ds(g * 2 * GROUP, 2 * GROUP), :] = pick
        PICKT[g] = pick.T
        part = dot(PICKT[g], rows[:, :ROW])
        total = part if total is None else total + part
    first_norm = sum_third(0)
    ray = ray / first_norm
    model_raw = [part / first_norm for part in by_parameter(total)]

    cell = [jnp.zeros((LOCAL, 128), F32) for _ in range(3)]
    direction = model = smooth = None
    phi_bar = first_norm
    rho_bar = u_norm = rho_now = sin_term = cos_term = None
    result = [jnp.zeros((LOCAL, 128), F32) for _ in range(3)]
    most, rest = range(GROUPS - 1), range(GROUPS - 1, GROUPS)
    for i in range(ITERS):
        e = 2 * i + 1
        final = i == ITERS - 1

        def beside_forward():
            for p in range(3):
                V[e - 1, p] = model_raw[p]
            sum_first(e, total_row(sum(v * v for v in model_raw)))
            send_halo(e - 1)

        send_forward(e, model_raw, beside_forward)
        smooth = laplace(e - 1)
        fetched = gather(e, S, most)
        v_norm = sum_third(e)
        model = [v / v_norm for v in model_raw]
        if i == 0:
            rho_bar = v_norm
            direction = model
        else:
            theta = sin_term * v_norm
            rho_bar = -cos_term * v_norm
            direction = [m - theta / rho_now * d for m, d in zip(model, direction)]
        cell_raw = [LAM * sm / v_norm - v_norm * q for sm, q in zip(smooth, cell)]
        cell_sum = total_row(sum(q * q for q in cell_raw))
        if not final:
            for p in range(3):
                V[e, p] = cell_raw[p]
            send_halo(e)
        scale = LIVE[...] / v_norm
        known = v_norm * ray
        FETCH[...] = gather(e, S, rest, fetched).astype(BF16)
        for t in range(TILES):
            row = forward_tile(t) * scale[t:t + 1] - known[t:t + 1]
            RAY[t:t + 1, :] = row
            if not final:
                adjoint_tile(t, row)

        def beside_adjoint():
            ray_raw = RAY[...]
            sum_first(e + 1, cell_sum + total_row(ray_raw * ray_raw))

        if not final:
            send_adjoint(e + 1, beside_adjoint)
            smooth = laplace(e)
            back = gather(e + 1, PICKT, most)
        else:
            beside_adjoint()
            sum_second(e + 1)
        u_norm = sum_third(e + 1)
        rho_now = jnp.sqrt(rho_bar * rho_bar + u_norm * u_norm)
        cos_term = rho_bar / rho_now
        sin_term = u_norm / rho_now
        phi_now = cos_term * phi_bar
        phi_bar = sin_term * phi_bar
        result = [r + phi_now / rho_now * d for r, d in zip(result, direction)]
        if not final:
            ray = RAY[...] / u_norm
            cell = [q / u_norm for q in cell_raw]
            known = [LAM * sm / u_norm - u_norm * m for sm, m in zip(smooth, model)]
            back = gather(e + 1, PICKT, rest, back)
            model_raw = [b / u_norm + k for b, k in zip(by_parameter(back), known)]

    for p in range(3):
        out_ref[p] = result[p]
    ratio_ref[...] = phi_bar / first_norm

    for e in range(EXCHANGES):
        wait_bytes(buffers(e)[0].at[pl.ds(0, DEVICES - 1)], xsend.at[e])
    for h in range(HALOS):
        for side in range(4):
            wait_bytes(HALO.at[h, side], hsend.at[h, side])
    for n in range(SUMS):
        wait_bytes(AY.at[n, pl.ds(0, 15)], s1.at[n])
        wait_bytes(AZ.at[n, pl.ds(0, 15)], s2.at[n])


def shards(weights, angles, block_list, observed, ray_count):
    ang = angles.transpose(0, 2, 1, 3).reshape(TILES, 3 * BLOCKS, 128)
    vmem = pl.BlockSpec(memory_space=pltpu.VMEM)
    dma = pltpu.SemaphoreType.DMA
    out, ratio = pl.pallas_call(
        kernel,
        out_shape=(
            jax.ShapeDtypeStruct((3, LOCAL, 128), F32),
            jax.ShapeDtypeStruct((1, 128), F32),
        ),
        in_specs=[pl.BlockSpec(memory_space=pl.ANY), vmem, vmem, vmem, pl.BlockSpec(memory_space=pltpu.SMEM)],
        out_specs=(vmem, vmem),
        scratch_shapes=[
            pltpu.VMEM((TILES, BLOCKS, 128, 128), BF16),
            pltpu.VMEM((TILES, BLOCKS * 128, 128), BF16),
            pltpu.VMEM((GROUPS, ENTRIES, 2 * GROUP), BF16),
            pltpu.VMEM((SLOTS, ENTRIES), BF16),
            pltpu.VMEM((SLOTS, ENTRIES), BF16),
            pltpu.VMEM((SLOTS, LOCAL), BF16),
            pltpu.VMEM((GROUPS, LOCAL, 2 * GROUP), BF16),
            pltpu.VMEM((TILES, 128), F32),
            pltpu.VMEM((3, ENTRIES, 128), F32),
            pltpu.VMEM((ENTRIES, ROW), BF16),
            pltpu.VMEM((TILES, 128), F32),
            pltpu.VMEM((DEVICES, 2, ROW + 128), BF16),
            pltpu.VMEM((DEVICES, 2, ROW + 128), BF16),
            pltpu.VMEM((EXCHANGES - 1, DEVICES, 2, ROW), BF16),
            pltpu.VMEM((EXCHANGES - 1, DEVICES, 2, ROW), BF16),
            pltpu.VMEM((HALOS, 3, LOCAL, 128), F32),
            pltpu.VMEM((HALOS, 2, 3, 8, 128), F32),
            pltpu.VMEM((HALOS, 4, 3, 8, 128), F32),
            pltpu.VMEM((SUMS, 2, 1, 128), F32),
            pltpu.VMEM((SUMS, 16, 1, 128), F32),
            pltpu.VMEM((SUMS, 16, 1, 128), F32),
            dma((TILES,)),
            dma((EXCHANGES,)),
            dma((EXCHANGES, GROUPS)),
            dma((HALOS, 4)),
            dma((HALOS, 4)),
            dma((SUMS,)),
            dma((SUMS,)),
            dma((SUMS,)),
            dma((SUMS,)),
            pltpu.SemaphoreType.REGULAR,
        ],
        compiler_params=pltpu.CompilerParams(
            collective_id=0, has_side_effects=True, vmem_limit_bytes=56 * 1024 * 1024
        ),
    )(weights, ang, block_list, observed, ray_count)
    out = out.reshape(3, 8, 8, 128).transpose(1, 2, 0, 3)
    return out, ratio[0, 0]


def solution(mesh):
    placed = (
        P(("slab", "lat"), None, None, None),
        P(("slab", "lat"), None, None, None),
        P(("slab", "lat"), None),
        P(("slab", "lat"), None),
        P("slab", "lat"),
    )
    return jax.shard_map(
        shards,
        mesh=mesh,
        in_specs=placed,
        out_specs=(P("slab", "lat", None, None), P()),
        check_vma=False,
    )
```

```python
import functools

import jax
import jax.numpy as jnp
from jax import lax
from jax.experimental import pallas as pl
from jax.experimental.pallas import tpu as pltpu
from jax.sharding import PartitionSpec as P

MESH = pl.DeviceIdType.MESH
F32 = jnp.float32
BF16 = jnp.bfloat16

TILES = 12
BLOCKS = 16
ENTRIES = TILES * BLOCKS
DEVICES = 256
CHIPS = 128
N_SLAB = 8
N_LAT = 32
SLOTS = 2 * DEVICES
LOCAL = 64
ROW = 384
ITERS = 3
GROUPS = 8

Z_HALVES = ((4, 5, 3, 6), (2, 7, 1, 0))


def ring(d, n):
    return min(d, n - d)


def block_order():
    blocks = [(dx, dy, half) for dx in range(4) for dy in range(4) for half in range(2)]

    def nearness(block):
        dx, dy, half = block
        far = ring(dx, 4) + ring(dy, 4) + (3, 1)[half]
        return (-far, half, (dx * 3 + dy * 5) % 7, dx, dy)

    return sorted(blocks, key=nearness)


ORDER = block_order()
GROUP = DEVICES // GROUPS
EXCHANGES = 2 * ITERS
HALOS = EXCHANGES - 1
SUMS = EXCHANGES + 1
SECOND_AT = 5
LAM = 0.3
EPS = 1e-6


def dot(a, b):
    return lax.dot_general(a, b, (((1,), (0,)), ((), ())), preferred_element_type=F32)


def iota(shape, dim):
    return lax.broadcasted_iota(jnp.int32, shape, dim).astype(F32)


def one_hot(same):
    return jnp.where(same, 1.0, 0.0).astype(BF16)


def wait_bytes(ref, sem):
    pltpu.make_async_copy(ref, ref, sem).wait()


def block_diagonal(rows):
    place = lax.broadcasted_iota(jnp.int32, rows.shape, 0) % BLOCKS
    empty = jnp.zeros_like(rows)
    return jnp.concatenate([jnp.where(place == k, rows, empty) for k in range(BLOCKS)], axis=1)


def kernel(
    w_hbm, ang_ref, ids_ref, obs_ref, cnt_ref, out_ref, ratio_ref,
    W, WT, S, ST, STL, PICK, PICKT, RAY, TRAV, PART, FETCH, LIVE,
    X0, R0, X, R, V, FACE, HALO, AX, AY, AZ, ALL,
    wsem, xsend, xrecv, hsend, hrecv, s1, r1, s2, r2, entered,
):
    s, l = lax.axis_index("slab"), lax.axis_index("lat")
    me = s * N_LAT + l
    y, c, z, x = lax.div(s, 2), lax.rem(s, 2), lax.div(l, 4), lax.rem(l, 4)
    a_me, b_me = z * 2 + c, y * 4 + x

    def a_dev(j):
        return (y * 2 + lax.rem(j, 2), lax.div(j, 2) * 4 + x)

    def b_dev(j):
        return (lax.div(j, 4) * 2 + c, z * 4 + lax.rem(j, 4))

    for t in range(TILES):
        pltpu.make_async_copy(w_hbm.at[t], W.at[t], wsem.at[t]).start()

    barrier = pltpu.get_barrier_semaphore()

    @pl.loop(1, 16)
    def _(j):
        pl.semaphore_signal(barrier, inc=1, device_id=a_dev(lax.rem(a_me + j, 16)), device_id_type=MESH)
        pl.semaphore_signal(barrier, inc=1, device_id=b_dev(lax.rem(b_me + j, 16)), device_id_type=MESH)

    spread_k = jnp.where(
        (lax.broadcasted_iota(jnp.int32, (BLOCKS, ENTRIES), 1) & (BLOCKS - 1))
        == lax.broadcasted_iota(jnp.int32, (BLOCKS, ENTRIES), 0),
        1.0, 0.0,
    ).astype(BF16)
    own_tile = (lax.broadcasted_iota(jnp.int32, (TILES, ENTRIES), 1) >> 4) == lax.broadcasted_iota(
        jnp.int32, (TILES, ENTRIES), 0
    )

    def in_a_row(values):
        spread = dot(values.astype(F32).astype(BF16), spread_k)
        return jnp.sum(jnp.where(own_tile, spread, 0.0), axis=0, keepdims=True).astype(jnp.int32)

    ids = ids_ref[...]
    depth, cross = in_a_row(ids >> 8), in_a_row(ids & 255)
    inner = (depth & 7) * 8 + (cross & 7)
    slab_o, lat_o = depth >> 3, cross >> 3
    dx, dz = ((lat_o & 3) - x) & 3, ((lat_o >> 2) - z) & 7
    dy, dc = ((slab_o >> 1) - y) & 3, ((slab_o & 1) - c) & 1

    half = jnp.zeros_like(dz)
    place_z = jnp.zeros_like(dz)
    for h in range(2):
        for k in range(4):
            half = jnp.where(dz == Z_HALVES[h][k], h, half)
            place_z = jnp.where(dz == Z_HALVES[h][k], k, place_z)
    code = (dx * 4 + dy) * 2 + half
    place_block = jnp.zeros_like(dz)
    for n, (bx, by, bh) in enumerate(ORDER):
        place_block = jnp.where(code == (bx * 4 + by) * 2 + bh, n, place_block)
    owner = place_block * 8 + (1 - dc) * 4 + place_z
    owner_r, inner_r = owner.astype(F32), inner.astype(F32)
    square = (ENTRIES, ENTRIES)
    i0, i1 = iota(square, 0), iota(square, 1)

    def column(row):
        return jnp.sum(jnp.where(i0 == i1, row, 0.0), axis=1, keepdims=True)

    owner_c, inner_c = column(owner_r), column(inner_r)
    same = jnp.where(owner_r == owner_c, 1.0, 0.0)
    slot_c = 2.0 * owner_c + jnp.sum(jnp.where(i1 < i0, same, 0.0), axis=1, keepdims=True)
    slot_r = 2.0 * owner_r + jnp.sum(jnp.where(i0 < i1, same, 0.0), axis=0, keepdims=True)
    alone = jnp.sum(same, axis=0, keepdims=True) == 1.0
    spare_r = jnp.where(alone, slot_r + 1.0, -1.0)
    for g in range(GROUPS):
        S[g] = one_hot(iota((ENTRIES, 2 * GROUP), 1) + float(2 * GROUP * g) == slot_c)
    st = one_hot(iota((SLOTS, ENTRIES), 0) == slot_r)
    stl = one_hot(iota((SLOTS, ENTRIES), 0) == spare_r)
    ST[...] = st
    STL[...] = stl
    wanted = dot(st + stl, one_hot(iota((ENTRIES, 128), 1) == inner_c)).astype(BF16)

    at = iota((TILES, 128), 0) * 128.0 + iota((TILES, 128), 1)
    LIVE[...] = jnp.where(at < cnt_ref[0, 0].astype(F32), 1.0, 0.0)

    def total_row(values):
        return jnp.sum(values, axis=0, keepdims=True)

    def sum_first(n, row):
        AX[n, 0] = row
        AY[n, a_me] = row

        @pl.loop(1, 16)
        def _(j):
            pltpu.make_async_remote_copy(
                AX.at[n, 0], AY.at[n, a_me], s1.at[n], r1.at[n],
                device_id=a_dev(lax.rem(a_me + j, 16)), device_id_type=MESH,
            ).start()

    def sum_second(n):
        wait_bytes(AY.at[n, pl.ds(0, 15)], r1.at[n])
        row = jnp.sum(AY[n], axis=0)
        AX[n, 1] = row
        AZ[n, b_me] = row

        @pl.loop(1, 16)
        def _(j):
            pltpu.make_async_remote_copy(
                AX.at[n, 1], AZ.at[n, b_me], s2.at[n], r2.at[n],
                device_id=b_dev(lax.rem(b_me + j, 16)), device_id_type=MESH,
            ).start()

    def sum_third(n):
        wait_bytes(AZ.at[n, pl.ds(0, 15)], r2.at[n])
        total = jnp.sum(jnp.sum(AZ[n], axis=0), axis=1, keepdims=True)
        return jnp.sqrt(jnp.broadcast_to(total, (1, 128)) + EPS)

    def sum_last(row):
        n = SUMS - 1
        AX[n, 0] = row
        pair = pltpu.make_async_remote_copy(
            AX.at[n, 0], AY.at[n, 0], s1.at[n], r1.at[n], device_id=(y * 2 + 1 - c, l), device_id_type=MESH
        )
        pair.start()
        pair.wait()
        row = row + AY[n, 0]
        AX[n, 1] = row
        ALL[CHIPS - 1] = row

        def one(j, to_y, to_x, dz):
            pltpu.make_async_remote_copy(
                AX.at[n, 1], ALL.at[j], s2.at[n], r2.at[n],
                device_id=(to_y * 2 + c, lax.rem(z + dz, 8) * 4 + to_x), device_id_type=MESH,
            ).start()

        def offset(i):
            far = 3 - i
            return lax.rem(lax.div(far * (far + 1), 2), 4)

        steps = Z_HALVES[0] + Z_HALVES[1]

        @pl.loop(0, 15)
        def _(q):
            to_x = lax.rem(x + offset(lax.div(q, 4)), 4)
            to_y = lax.rem(y + offset(lax.rem(q, 4)), 4)
            for k in range(8):
                one(q * 8 + k, to_y, to_x, steps[k])

        for k in range(7):
            one(120 + k, y, x, steps[k])
        wait_bytes(ALL.at[pl.ds(0, CHIPS - 1)], r2.at[n])
        total = jnp.sum(jnp.sum(ALL[...], axis=0), axis=1, keepdims=True)
        return jnp.sqrt(jnp.broadcast_to(total, (1, 128)) + EPS)

    def buffers(e):
        return (X0, R0) if e == 0 else (X.at[e - 1], R.at[e - 1])

    def send_group(e, g, forward):
        src, dst = buffers(e)
        blocks = ORDER[g * 4:(g + 1) * 4]

        def of_block(b, values):
            value = values[0]
            for n in range(1, 4):
                value = jnp.where(b == n, values[n], value)
            return value

        def place(at, d, n):
            return lax.rem(at + n - d, n) if forward else lax.rem(at + d, n)

        def one(i, k, to_z, to_x, to_slab):
            j = g * GROUP + i * 4 + k
            pltpu.make_async_remote_copy(
                src.at[j], dst.at[j], xsend.at[e], xrecv.at[e, g],
                device_id=(to_slab, to_z * 4 + to_x), device_id_type=MESH,
            ).start()

        @pl.loop(0, 7 if g == GROUPS - 1 else 8)
        def _(i):
            b = lax.div(i, 2)
            to_x = place(x, of_block(b, [n[0] for n in blocks]), 4)
            to_y = place(y, of_block(b, [n[1] for n in blocks]), 4)
            to_c = lax.rem(c + 1 - lax.rem(i, 2), 2)
            for k in range(4):
                dz = of_block(b, [Z_HALVES[n[2]][k] for n in blocks])
                one(i, k, place(z, dz, 8), to_x, to_y * 2 + to_c)

        if g == GROUPS - 1:
            for k in range(3):
                one(7, k, place(z, Z_HALVES[1][k], 8), x, s)
            pltpu.make_async_copy(src.at[DEVICES - 1], dst.at[DEVICES - 1], xrecv.at[e, g]).start()

    def receive_group(e, g):
        dst = buffers(e)[1].at[pl.ds(g * GROUP, GROUP)]
        wait_bytes(dst, xrecv.at[e, g])
        return dst[...].reshape(2 * GROUP, dst.shape[-1])

    def send_halo(h):
        for p in range(3):
            v = V[h, p]
            FACE[h, 0, p] = jnp.concatenate([v[8 * i:8 * i + 1] for i in range(8)], axis=0)
            FACE[h, 1, p] = jnp.concatenate([v[8 * i + 7:8 * i + 8] for i in range(8)], axis=0)
        before, after = lax.rem(s + N_SLAB - 1, N_SLAB), lax.rem(s + 1, N_SLAB)
        left, right = lax.rem(l + N_LAT - 1, N_LAT), lax.rem(l + 1, N_LAT)
        moves = (
            (V.at[h, :, pl.ds(56, 8)], 0, (after, l)),
            (V.at[h, :, pl.ds(0, 8)], 1, (before, l)),
            (FACE.at[h, 1], 2, (s, right)),
            (FACE.at[h, 0], 3, (s, left)),
        )
        for src, side, device in moves:
            pltpu.make_async_remote_copy(
                src, HALO.at[h, side], hsend.at[h, side], hrecv.at[h, side],
                device_id=device, device_id_type=MESH,
            ).start()

    def laplace(h):
        for side in range(4):
            wait_bytes(HALO.at[h, side], hrecv.at[h, side])
        row = lax.broadcasted_iota(jnp.int32, (LOCAL, 128), 0) % 8
        lane = lax.broadcasted_iota(jnp.int32, (LOCAL, 128), 1)

        def spread(face):
            return jnp.concatenate([jnp.broadcast_to(face[i:i + 1], (8, 128)) for i in range(8)], axis=0)

        result = []
        for p in range(3):
            v = V[h, p]
            low = jnp.where(s > 0, HALO[h, 0, p], 0.0)
            high = jnp.where(s < N_SLAB - 1, HALO[h, 1, p], 0.0)
            left = jnp.where(l > 0, HALO[h, 2, p], 0.0)
            right = jnp.where(l < N_LAT - 1, HALO[h, 3, p], 0.0)
            beside = jnp.concatenate([low, v[:56]], axis=0) + jnp.concatenate([v[8:], high], axis=0)
            beside = beside + jnp.where(row == 0, spread(left), pltpu.roll(v, 1, 0))
            beside = beside + jnp.where(row == 7, spread(right), pltpu.roll(v, LOCAL - 1, 0))
            beside = beside + jnp.where(lane == 0, 0.0, pltpu.roll(v, 1, 1))
            beside = beside + jnp.where(lane == 127, 0.0, pltpu.roll(v, 127, 1))
            result.append(6.0 * v - beside)
        return result

    def forward_tile(t):
        rows = jnp.concatenate(
            [FETCH[t * BLOCKS:(t + 1) * BLOCKS, p * 128:(p + 1) * 128] for p in range(3)], axis=0
        )
        return total_row(dot(block_diagonal(rows), WT[t]) * ang_ref[t])

    def adjoint_tile(t, ray_row):
        weighted = ang_ref[t] * ray_row
        high = weighted.astype(BF16)
        low = (weighted - high.astype(F32)).astype(BF16)
        rows = block_diagonal(jnp.concatenate([high, low], axis=0))
        out = dot(rows, W[t].reshape(BLOCKS * 128, 128))
        out = out[:48] + out[48:]
        for p in range(3):
            PART[p, t * BLOCKS:(t + 1) * BLOCKS, :] = out[p * BLOCKS:(p + 1) * BLOCKS]

    def send_adjoint(e, beside):
        high = [PART[p].astype(BF16) for p in range(3)]
        low = [(PART[p] - high[p].astype(F32)).astype(BF16) for p in range(3)]
        high, low = jnp.concatenate(high, axis=1), jnp.concatenate(low, axis=1)
        for g in range(GROUPS):
            at = pl.ds(g * 2 * GROUP, 2 * GROUP)
            rows = (dot(ST[at, :], high) + dot(STL[at, :], low)).astype(BF16)
            if e == 0:
                rows = jnp.concatenate([rows, wanted[g * 2 * GROUP:(g + 1) * 2 * GROUP]], axis=1)
            src = buffers(e)[0]
            src[pl.ds(g * GROUP, GROUP)] = rows.reshape(GROUP, 2, rows.shape[-1])
            if g == 0:
                beside()
            send_group(e, g, False)
            if g == SECOND_AT:
                sum_second(e)

    def send_forward(e, values):
        model = jnp.concatenate(values, axis=1).astype(BF16)
        for g in range(GROUPS):
            rows = dot(PICK[pl.ds(g * 2 * GROUP, 2 * GROUP), :], model).astype(BF16)
            buffers(e)[0][pl.ds(g * GROUP, GROUP)] = rows.reshape(GROUP, 2, ROW)
            if g == 0:
                sum_first(e, total_row(sum(v * v for v in values)))
            send_group(e, g, True)
            if g == 1:
                send_halo(e - 1)
            if g == SECOND_AT:
                sum_second(e)

    def gather(e, table, groups, total=None):
        for g in groups:
            part = dot(table[g], receive_group(e, g))
            total = part if total is None else total + part
        return total

    def by_parameter(total):
        return [total[:, p * 128:(p + 1) * 128] for p in range(3)]

    ray = obs_ref[...] * LIVE[...]
    RAY[...] = ray
    pl.semaphore_wait(barrier, 30)

    @pl.loop(1, 16)
    def _(j):
        pl.semaphore_signal(entered, inc=1, device_id=b_dev(lax.rem(b_me + j, 16)), device_id_type=MESH)

    for t in range(TILES):
        wait_bytes(W.at[t], wsem.at[t])
        adjoint_tile(t, RAY[t:t + 1, :])
    pl.semaphore_wait(entered, 15)
    send_adjoint(0, lambda: sum_first(0, total_row(ray * ray)))

    def turn(t, carry):
        for k in range(BLOCKS):
            WT[t, k * 128:(k + 1) * 128, :] = W[t, k].T
        return carry

    lax.fori_loop(0, TILES, turn, 0)
    total = None
    for g in range(GROUPS):
        rows = receive_group(0, g)
        pick = rows[:, ROW:ROW + LOCAL]
        PICK[pl.ds(g * 2 * GROUP, 2 * GROUP), :] = pick
        PICKT[g] = pick.T
        part = dot(PICKT[g], rows[:, :ROW])
        total = part if total is None else total + part
    first_norm = sum_third(0)
    ray = ray / first_norm
    model_raw = [part / first_norm for part in by_parameter(total)]

    cell = [jnp.zeros((LOCAL, 128), F32) for _ in range(3)]
    direction = model = smooth = None
    phi_bar = first_norm
    rho_bar = u_norm = rho_now = sin_term = cos_term = None
    result = [jnp.zeros((LOCAL, 128), F32) for _ in range(3)]
    most, rest = range(GROUPS - 1), range(GROUPS - 1, GROUPS)
    for i in range(ITERS):
        e = 2 * i + 1
        final = i == ITERS - 1

        for p in range(3):
            V[e - 1, p] = model_raw[p]
        send_forward(e, model_raw)
        smooth = laplace(e - 1)
        fetched = gather(e, S, most)
        v_norm = sum_third(e)
        model = [v / v_norm for v in model_raw]
        if i == 0:
            rho_bar = v_norm
            direction = model
        else:
            theta = sin_term * v_norm
            rho_bar = -cos_term * v_norm
            direction = [m - theta / rho_now * d for m, d in zip(model, direction)]
        cell_raw = [LAM * sm / v_norm - v_norm * q for sm, q in zip(smooth, cell)]
        cell_sum = total_row(sum(q * q for q in cell_raw))
        if not final:
            for p in range(3):
                V[e, p] = cell_raw[p]
            send_halo(e)
        scale = LIVE[...] / v_norm
        known = v_norm * ray
        FETCH[...] = gather(e, S, rest, fetched).astype(BF16)
        for t in range(TILES):
            TRAV[t:t + 1, :] = forward_tile(t)
        ray_raw = TRAV[...] * scale - known
        RAY[...] = ray_raw
        for t in range(0 if final else TILES):
            adjoint_tile(t, RAY[t:t + 1, :])

        ray_sum = cell_sum + total_row(ray_raw * ray_raw)

        if not final:
            send_adjoint(e + 1, lambda: sum_first(e + 1, ray_sum))
            smooth = laplace(e)
            back = gather(e + 1, PICKT, most)
            u_norm = sum_third(e + 1)
        else:
            u_norm = sum_last(ray_sum)
        rho_now = jnp.sqrt(rho_bar * rho_bar + u_norm * u_norm)
        cos_term = rho_bar / rho_now
        sin_term = u_norm / rho_now
        phi_now = cos_term * phi_bar
        phi_bar = sin_term * phi_bar
        result = [r + phi_now / rho_now * d for r, d in zip(result, direction)]
        if not final:
            ray = ray_raw / u_norm
            cell = [q / u_norm for q in cell_raw]
            known = [LAM * sm / u_norm - u_norm * m for sm, m in zip(smooth, model)]
            back = gather(e + 1, PICKT, rest, back)
            model_raw = [b / u_norm + k for b, k in zip(by_parameter(back), known)]

    for p in range(3):
        out_ref[p] = result[p]
    ratio_ref[...] = phi_bar / first_norm

    for e in range(EXCHANGES):
        wait_bytes(buffers(e)[0].at[pl.ds(0, DEVICES - 1)], xsend.at[e])
    for h in range(HALOS):
        for side in range(4):
            wait_bytes(HALO.at[h, side], hsend.at[h, side])
    for n in range(SUMS - 1):
        wait_bytes(AY.at[n, pl.ds(0, 15)], s1.at[n])
        wait_bytes(AZ.at[n, pl.ds(0, 15)], s2.at[n])
    wait_bytes(ALL.at[pl.ds(0, CHIPS - 1)], s2.at[SUMS - 1])


def shards(weights, angles, block_list, observed, ray_count):
    ang = angles.transpose(0, 2, 1, 3).reshape(TILES, 3 * BLOCKS, 128)
    vmem = pl.BlockSpec(memory_space=pltpu.VMEM)
    dma = pltpu.SemaphoreType.DMA
    out, ratio = pl.pallas_call(
        kernel,
        out_shape=(
            jax.ShapeDtypeStruct((3, LOCAL, 128), F32),
            jax.ShapeDtypeStruct((1, 128), F32),
        ),
        in_specs=[pl.BlockSpec(memory_space=pl.ANY), vmem, vmem, vmem, pl.BlockSpec(memory_space=pltpu.SMEM)],
        out_specs=(vmem, vmem),
        scratch_shapes=[
            pltpu.VMEM((TILES, BLOCKS, 128, 128), BF16),
            pltpu.VMEM((TILES, BLOCKS * 128, 128), BF16),
            pltpu.VMEM((GROUPS, ENTRIES, 2 * GROUP), BF16),
            pltpu.VMEM((SLOTS, ENTRIES), BF16),
            pltpu.VMEM((SLOTS, ENTRIES), BF16),
            pltpu.VMEM((SLOTS, LOCAL), BF16),
            pltpu.VMEM((GROUPS, LOCAL, 2 * GROUP), BF16),
            pltpu.VMEM((TILES, 128), F32),
            pltpu.VMEM((TILES, 128), F32),
            pltpu.VMEM((3, ENTRIES, 128), F32),
            pltpu.VMEM((ENTRIES, ROW), BF16),
            pltpu.VMEM((TILES, 128), F32),
            pltpu.VMEM((DEVICES, 2, ROW + 128), BF16),
            pltpu.VMEM((DEVICES, 2, ROW + 128), BF16),
            pltpu.VMEM((EXCHANGES - 1, DEVICES, 2, ROW), BF16),
            pltpu.VMEM((EXCHANGES - 1, DEVICES, 2, ROW), BF16),
            pltpu.VMEM((HALOS, 3, LOCAL, 128), F32),
            pltpu.VMEM((HALOS, 2, 3, 8, 128), F32),
            pltpu.VMEM((HALOS, 4, 3, 8, 128), F32),
            pltpu.VMEM((SUMS, 2, 1, 128), F32),
            pltpu.VMEM((SUMS, 16, 1, 128), F32),
            pltpu.VMEM((SUMS, 16, 1, 128), F32),
            pltpu.VMEM((CHIPS, 1, 128), F32),
            dma((TILES,)),
            dma((EXCHANGES,)),
            dma((EXCHANGES, GROUPS)),
            dma((HALOS, 4)),
            dma((HALOS, 4)),
            dma((SUMS,)),
            dma((SUMS,)),
            dma((SUMS,)),
            dma((SUMS,)),
            pltpu.SemaphoreType.REGULAR,
        ],
        compiler_params=pltpu.CompilerParams(
            collective_id=0, has_side_effects=True, vmem_limit_bytes=56 * 1024 * 1024
        ),
    )(weights, ang, block_list, observed, ray_count)
    out = out.reshape(3, 8, 8, 128).transpose(1, 2, 0, 3)
    return out, ratio[0, 0]


def solution(mesh):
    placed = (
        P(("slab", "lat"), None, None, None),
        P(("slab", "lat"), None, None, None),
        P(("slab", "lat"), None),
        P(("slab", "lat"), None),
        P("slab", "lat"),
    )
    return jax.shard_map(
        shards,
        mesh=mesh,
        in_specs=placed,
        out_specs=(P("slab", "lat", None, None), P()),
        check_vma=False,
    )
```

```python
import functools

import jax
import jax.numpy as jnp
from jax import lax
from jax.experimental import pallas as pl
from jax.experimental.pallas import tpu as pltpu
from jax.sharding import PartitionSpec as P

MESH = pl.DeviceIdType.MESH
F32 = jnp.float32
BF16 = jnp.bfloat16

TILES = 12
BLOCKS = 16
ENTRIES = TILES * BLOCKS
DEVICES = 256
CHIPS = 128
N_SLAB = 8
N_LAT = 32
SLOTS = 2 * DEVICES
LOCAL = 64
ROW = 384
ITERS = 3
GROUPS = 8

Z_HALVES = ((4, 5, 3, 6), (2, 7, 1, 0))


def ring(d, n):
    return min(d, n - d)


def block_order():
    blocks = [(dx, dy, half) for dx in range(4) for dy in range(4) for half in range(2)]

    def nearness(block):
        dx, dy, half = block
        far = ring(dx, 4) + ring(dy, 4) + (3, 1)[half]
        return (-far, half, (dx * 3 + dy * 5) % 7, dx, dy)

    return sorted(blocks, key=nearness)


ORDER = block_order()
GROUP = DEVICES // GROUPS
EXCHANGES = 2 * ITERS
HALOS = EXCHANGES - 1
SUMS = EXCHANGES + 1
SECOND_AT = 5
LAM = 0.3
EPS = 1e-6


def dot(a, b):
    return lax.dot_general(a, b, (((1,), (0,)), ((), ())), preferred_element_type=F32)


def iota(shape, dim):
    return lax.broadcasted_iota(jnp.int32, shape, dim).astype(F32)


def one_hot(same):
    return jnp.where(same, 1.0, 0.0).astype(BF16)


def wait_bytes(ref, sem):
    pltpu.make_async_copy(ref, ref, sem).wait()


def block_diagonal(rows):
    place = lax.broadcasted_iota(jnp.int32, rows.shape, 0) % BLOCKS
    empty = jnp.zeros_like(rows)
    return jnp.concatenate([jnp.where(place == k, rows, empty) for k in range(BLOCKS)], axis=1)


def kernel(
    w_hbm, ang_hbm, ids_hbm, obs_hbm, cnt_hbm, out_hbm, ratio_hbm,
    ang_ref, ids_ref, obs_ref, cnt_ref, out_ref, ratio_ref,
    W, WT, S, ST, STL, PICK, PICKT, RAY, TRAV, PART, FETCH, LIVE,
    X, R, V, FACE, HALO, AX, AY, AZ, ALL, ASK, ASKED,
    wsem, xsend, xrecv, hsend, hrecv, s1, r1, s2, r2, q1, q2, isem, entered,
):
    s, l = lax.axis_index("slab"), lax.axis_index("lat")
    me = s * N_LAT + l
    y, c, z, x = lax.div(s, 2), lax.rem(s, 2), lax.div(l, 4), lax.rem(l, 4)
    a_me, b_me = z * 2 + c, y * 4 + x

    def a_dev(j):
        return (y * 2 + lax.rem(j, 2), lax.div(j, 2) * 4 + x)

    def b_dev(j):
        return (lax.div(j, 4) * 2 + c, z * 4 + lax.rem(j, 4))

    operands = [
        pltpu.make_async_copy(src, dst, isem.at[n])
        for n, (src, dst) in enumerate(
            ((ids_hbm, ids_ref), (cnt_hbm, cnt_ref), (obs_hbm, obs_ref), (ang_hbm, ang_ref))
        )
    ]

    barrier = pltpu.get_barrier_semaphore()

    @pl.loop(1, 16)
    def _(j):
        pl.semaphore_signal(barrier, inc=1, device_id=a_dev(lax.rem(a_me + j, 16)), device_id_type=MESH)
        pl.semaphore_signal(barrier, inc=1, device_id=b_dev(lax.rem(b_me + j, 16)), device_id_type=MESH)

    for copy in operands:
        copy.start()
    for t in range(TILES):
        pltpu.make_async_copy(w_hbm.at[t], W.at[t], wsem.at[t]).start()
    operands[0].wait()

    spread_k = jnp.where(
        (lax.broadcasted_iota(jnp.int32, (BLOCKS, ENTRIES), 1) & (BLOCKS - 1))
        == lax.broadcasted_iota(jnp.int32, (BLOCKS, ENTRIES), 0),
        1.0, 0.0,
    ).astype(BF16)
    own_tile = (lax.broadcasted_iota(jnp.int32, (TILES, ENTRIES), 1) >> 4) == lax.broadcasted_iota(
        jnp.int32, (TILES, ENTRIES), 0
    )

    def in_a_row(values):
        spread = dot(values.astype(F32).astype(BF16), spread_k)
        return jnp.sum(jnp.where(own_tile, spread, 0.0), axis=0, keepdims=True).astype(jnp.int32)

    ids = ids_ref[...]
    depth, cross = in_a_row(ids >> 8), in_a_row(ids & 255)
    inner = (depth & 7) * 8 + (cross & 7)
    slab_o, lat_o = depth >> 3, cross >> 3
    dx, dz = ((lat_o & 3) - x) & 3, ((lat_o >> 2) - z) & 7
    dy, dc = ((slab_o >> 1) - y) & 3, ((slab_o & 1) - c) & 1

    half = jnp.zeros_like(dz)
    place_z = jnp.zeros_like(dz)
    for h in range(2):
        for k in range(4):
            half = jnp.where(dz == Z_HALVES[h][k], h, half)
            place_z = jnp.where(dz == Z_HALVES[h][k], k, place_z)
    code = (dx * 4 + dy) * 2 + half
    place_block = jnp.zeros_like(dz)
    for n, (bx, by, bh) in enumerate(ORDER):
        place_block = jnp.where(code == (bx * 4 + by) * 2 + bh, n, place_block)
    owner = place_block * 8 + (1 - dc) * 4 + place_z
    owner_r, inner_r = owner.astype(F32), inner.astype(F32)
    square = (ENTRIES, ENTRIES)
    i0, i1 = iota(square, 0), iota(square, 1)

    def column(row):
        return jnp.sum(jnp.where(i0 == i1, row, 0.0), axis=1, keepdims=True)

    owner_c, inner_c = column(owner_r), column(inner_r)
    same = jnp.where(owner_r == owner_c, 1.0, 0.0)
    slot_c = 2.0 * owner_c + jnp.sum(jnp.where(i1 < i0, same, 0.0), axis=1, keepdims=True)
    slot_r = 2.0 * owner_r + jnp.sum(jnp.where(i0 < i1, same, 0.0), axis=0, keepdims=True)
    alone = jnp.sum(same, axis=0, keepdims=True) == 1.0
    spare_r = jnp.where(alone, slot_r + 1.0, -1.0)
    for g in range(GROUPS):
        S[g] = one_hot(iota((ENTRIES, 2 * GROUP), 1) + float(2 * GROUP * g) == slot_c)
    st = one_hot(iota((SLOTS, ENTRIES), 0) == slot_r)
    stl = one_hot(iota((SLOTS, ENTRIES), 0) == spare_r)
    ST[...] = st
    STL[...] = stl

    rank_r = slot_r - 2.0 * owner_r
    a_r = ((lat_o >> 2) * 2 + (slab_o & 1)).astype(F32)
    lane_r = 2.0 * ((slab_o >> 1) * 4 + (lat_o & 3)).astype(F32) + rank_r
    lane_c = column(lane_r)
    spare_c = column(jnp.where(alone, lane_r + 1.0, -1.0))
    lanes = iota((ENTRIES, 128), 1)
    asked = dot(
        jnp.where(iota((16, ENTRIES), 0) == a_r, inner_r + 1.0, 0.0).astype(BF16),
        one_hot(lanes == lane_c) + one_hot(lanes == spare_c),
    )

    def ask_first():
        for i in range(16):
            ASK[0, i] = asked[i:i + 1]
        ASKED[0, a_me] = ASK[0, a_me]

        @pl.loop(1, 16)
        def _(j):
            d = lax.rem(a_me + j, 16)
            pltpu.make_async_remote_copy(
                ASK.at[0, d], ASKED.at[0, a_me], q1.at[0], q1.at[1], device_id=a_dev(d), device_id_type=MESH
            ).start()

    def ask_second():
        wait_bytes(ASKED.at[0, pl.ds(0, 15)], q1.at[1])
        rows = jnp.concatenate([ASKED[0, i] for i in range(16)], axis=0).astype(BF16)
        turned = None
        for r in range(2):
            mine = one_hot(iota((16, 128), 1) == 2.0 * iota((16, 128), 0) + float(r))
            part = lax.dot_general(mine, rows, (((1,), (1,)), ((), ())), preferred_element_type=F32)
            part = dot(part.astype(BF16), mine)
            turned = part if turned is None else turned + part
        for i in range(16):
            ASK[1, i] = turned[i:i + 1]
        ASKED[1, b_me] = ASK[1, b_me]

        @pl.loop(1, 16)
        def _(j):
            d = lax.rem(b_me + j, 16)
            pltpu.make_async_remote_copy(
                ASK.at[1, d], ASKED.at[1, b_me], q2.at[0], q2.at[1], device_id=b_dev(d), device_id_type=MESH
            ).start()

    def ask_third():
        slot = lax.broadcasted_iota(jnp.int32, (1, SLOTS), 1)
        block, core, k = slot >> 4, (slot >> 3) & 1, (slot >> 1) & 3
        from_x, from_y, half = jnp.zeros_like(slot), jnp.zeros_like(slot), jnp.zeros_like(slot)
        for n, (bx, by, bh) in enumerate(ORDER):
            here = block == n
            from_x = jnp.where(here, (x - bx) & 3, from_x)
            from_y = jnp.where(here, (y - by) & 3, from_y)
            half = jnp.where(here, bh, half)
        from_z = jnp.zeros_like(slot)
        for h in range(2):
            for n in range(4):
                from_z = jnp.where(half * 4 + k == h * 4 + n, (z - Z_HALVES[h][n]) & 7, from_z)
        from_c = (c + 1 - core) & 1
        a_s = (from_z * 2 + from_c).astype(F32)
        b_s = (from_y * 4 + from_x).astype(F32)
        lane_s = 2.0 * a_s + (slot & 1).astype(F32)
        lane_table = one_hot(iota((128, SLOTS), 0) == lane_s)
        wait_bytes(ASKED.at[1, pl.ds(0, 15)], q2.at[1])
        rows = jnp.concatenate([ASKED[1, i] for i in range(16)], axis=0).astype(BF16)
        found = jnp.where(iota((16, SLOTS), 0) == b_s, dot(rows, lane_table), 0.0)
        inner_s = jnp.sum(found, axis=0, keepdims=True) - 1.0
        picked = jnp.where(iota((LOCAL, SLOTS), 0) == inner_s, 1.0, 0.0)
        PICK[...] = picked.T.astype(BF16)
        for g in range(GROUPS):
            PICKT[g] = PICK[pl.ds(g * 2 * GROUP, 2 * GROUP), :].T


    at = iota((TILES, 128), 0) * 128.0 + iota((TILES, 128), 1)
    operands[1].wait()
    LIVE[...] = jnp.where(at < cnt_ref[...].astype(F32), 1.0, 0.0)

    def total_row(values):
        return jnp.sum(values, axis=0, keepdims=True)

    def sum_first(n, row):
        AX[n, 0] = row
        AY[n, a_me] = row

        @pl.loop(1, 16)
        def _(j):
            pltpu.make_async_remote_copy(
                AX.at[n, 0], AY.at[n, a_me], s1.at[n], r1.at[n],
                device_id=a_dev(lax.rem(a_me + j, 16)), device_id_type=MESH,
            ).start()

    def sum_second(n):
        wait_bytes(AY.at[n, pl.ds(0, 15)], r1.at[n])
        row = jnp.sum(AY[n], axis=0)
        AX[n, 1] = row
        AZ[n, b_me] = row

        @pl.loop(1, 16)
        def _(j):
            pltpu.make_async_remote_copy(
                AX.at[n, 1], AZ.at[n, b_me], s2.at[n], r2.at[n],
                device_id=b_dev(lax.rem(b_me + j, 16)), device_id_type=MESH,
            ).start()

    def sum_third(n):
        wait_bytes(AZ.at[n, pl.ds(0, 15)], r2.at[n])
        total = jnp.sum(jnp.sum(AZ[n], axis=0), axis=1, keepdims=True)
        return jnp.sqrt(jnp.broadcast_to(total, (1, 128)) + EPS)

    def sum_last(row):
        n = SUMS - 1
        AX[n, 0] = row
        pair = pltpu.make_async_remote_copy(
            AX.at[n, 0], AY.at[n, 0], s1.at[n], r1.at[n], device_id=(y * 2 + 1 - c, l), device_id_type=MESH
        )
        pair.start()
        pair.wait()
        row = row + AY[n, 0]
        AX[n, 1] = row
        ALL[CHIPS - 1] = row

        def one(j, to_y, to_x, dz):
            pltpu.make_async_remote_copy(
                AX.at[n, 1], ALL.at[j], s2.at[n], r2.at[n],
                device_id=(to_y * 2 + c, lax.rem(z + dz, 8) * 4 + to_x), device_id_type=MESH,
            ).start()

        def offset(i):
            far = 3 - i
            return lax.rem(lax.div(far * (far + 1), 2), 4)

        steps = Z_HALVES[0] + Z_HALVES[1]

        @pl.loop(0, 15)
        def _(q):
            to_x = lax.rem(x + offset(lax.div(q, 4)), 4)
            to_y = lax.rem(y + offset(lax.rem(q, 4)), 4)
            for k in range(8):
                one(q * 8 + k, to_y, to_x, steps[k])

        for k in range(7):
            one(120 + k, y, x, steps[k])
        wait_bytes(ALL.at[pl.ds(0, CHIPS - 1)], r2.at[n])
        total = jnp.sum(jnp.sum(ALL[...], axis=0), axis=1, keepdims=True)
        return jnp.sqrt(jnp.broadcast_to(total, (1, 128)) + EPS)

    def buffers(e):
        return X.at[e], R.at[e]

    def send_group(e, g, forward):
        src, dst = buffers(e)
        blocks = ORDER[g * 4:(g + 1) * 4]

        def of_block(b, values):
            value = values[0]
            for n in range(1, 4):
                value = jnp.where(b == n, values[n], value)
            return value

        def place(at, d, n):
            return lax.rem(at + n - d, n) if forward else lax.rem(at + d, n)

        def one(i, k, to_z, to_x, to_slab):
            j = g * GROUP + i * 4 + k
            pltpu.make_async_remote_copy(
                src.at[j], dst.at[j], xsend.at[e], xrecv.at[e, g],
                device_id=(to_slab, to_z * 4 + to_x), device_id_type=MESH,
            ).start()

        @pl.loop(0, 7 if g == GROUPS - 1 else 8)
        def _(i):
            b = lax.div(i, 2)
            to_x = place(x, of_block(b, [n[0] for n in blocks]), 4)
            to_y = place(y, of_block(b, [n[1] for n in blocks]), 4)
            to_c = lax.rem(c + 1 - lax.rem(i, 2), 2)
            for k in range(4):
                dz = of_block(b, [Z_HALVES[n[2]][k] for n in blocks])
                one(i, k, place(z, dz, 8), to_x, to_y * 2 + to_c)

        if g == GROUPS - 1:
            for k in range(3):
                one(7, k, place(z, Z_HALVES[1][k], 8), x, s)
            pltpu.make_async_copy(src.at[DEVICES - 1], dst.at[DEVICES - 1], xrecv.at[e, g]).start()

    def receive_group(e, g):
        dst = buffers(e)[1].at[pl.ds(g * GROUP, GROUP)]
        wait_bytes(dst, xrecv.at[e, g])
        return dst[...].reshape(2 * GROUP, dst.shape[-1])

    def send_halo(h):
        for p in range(3):
            v = V[h, p]
            FACE[h, 0, p] = jnp.concatenate([v[8 * i:8 * i + 1] for i in range(8)], axis=0)
            FACE[h, 1, p] = jnp.concatenate([v[8 * i + 7:8 * i + 8] for i in range(8)], axis=0)
        before, after = lax.rem(s + N_SLAB - 1, N_SLAB), lax.rem(s + 1, N_SLAB)
        left, right = lax.rem(l + N_LAT - 1, N_LAT), lax.rem(l + 1, N_LAT)
        moves = (
            (V.at[h, :, pl.ds(56, 8)], 0, (after, l)),
            (V.at[h, :, pl.ds(0, 8)], 1, (before, l)),
            (FACE.at[h, 1], 2, (s, right)),
            (FACE.at[h, 0], 3, (s, left)),
        )
        for src, side, device in moves:
            pltpu.make_async_remote_copy(
                src, HALO.at[h, side], hsend.at[h, side], hrecv.at[h, side],
                device_id=device, device_id_type=MESH,
            ).start()

    def laplace(h):
        for side in range(4):
            wait_bytes(HALO.at[h, side], hrecv.at[h, side])
        row = lax.broadcasted_iota(jnp.int32, (LOCAL, 128), 0) % 8
        lane = lax.broadcasted_iota(jnp.int32, (LOCAL, 128), 1)

        def spread(face):
            return jnp.concatenate([jnp.broadcast_to(face[i:i + 1], (8, 128)) for i in range(8)], axis=0)

        result = []
        for p in range(3):
            v = V[h, p]
            low = jnp.where(s > 0, HALO[h, 0, p], 0.0)
            high = jnp.where(s < N_SLAB - 1, HALO[h, 1, p], 0.0)
            left = jnp.where(l > 0, HALO[h, 2, p], 0.0)
            right = jnp.where(l < N_LAT - 1, HALO[h, 3, p], 0.0)
            beside = jnp.concatenate([low, v[:56]], axis=0) + jnp.concatenate([v[8:], high], axis=0)
            beside = beside + jnp.where(row == 0, spread(left), pltpu.roll(v, 1, 0))
            beside = beside + jnp.where(row == 7, spread(right), pltpu.roll(v, LOCAL - 1, 0))
            beside = beside + jnp.where(lane == 0, 0.0, pltpu.roll(v, 1, 1))
            beside = beside + jnp.where(lane == 127, 0.0, pltpu.roll(v, 127, 1))
            result.append(6.0 * v - beside)
        return result

    def forward_tile(t):
        rows = jnp.concatenate(
            [FETCH[t * BLOCKS:(t + 1) * BLOCKS, p * 128:(p + 1) * 128] for p in range(3)], axis=0
        )
        return total_row(dot(block_diagonal(rows), WT[t]) * ang_ref[t])

    def adjoint_tile(t, ray_row):
        weighted = ang_ref[t] * ray_row
        high = weighted.astype(BF16)
        low = (weighted - high.astype(F32)).astype(BF16)
        rows = block_diagonal(jnp.concatenate([high, low], axis=0))
        out = dot(rows, W[t].reshape(BLOCKS * 128, 128))
        out = out[:48] + out[48:]
        for p in range(3):
            PART[p, t * BLOCKS:(t + 1) * BLOCKS, :] = out[p * BLOCKS:(p + 1) * BLOCKS]

    def send_adjoint(e, beside):
        high = [PART[p].astype(BF16) for p in range(3)]
        low = [(PART[p] - high[p].astype(F32)).astype(BF16) for p in range(3)]
        high, low = jnp.concatenate(high, axis=1), jnp.concatenate(low, axis=1)
        for g in range(GROUPS):
            at = pl.ds(g * 2 * GROUP, 2 * GROUP)
            rows = (dot(ST[at, :], high) + dot(STL[at, :], low)).astype(BF16)
            src = buffers(e)[0]
            src[pl.ds(g * GROUP, GROUP)] = rows.reshape(GROUP, 2, rows.shape[-1])
            if g == 0:
                beside()
            send_group(e, g, False)
            if g == SECOND_AT:
                sum_second(e)

    def send_forward(e, values):
        model = jnp.concatenate(values, axis=1).astype(BF16)
        for g in range(GROUPS):
            rows = dot(PICK[pl.ds(g * 2 * GROUP, 2 * GROUP), :], model).astype(BF16)
            buffers(e)[0][pl.ds(g * GROUP, GROUP)] = rows.reshape(GROUP, 2, ROW)
            if g == 0:
                sum_first(e, total_row(sum(v * v for v in values)))
            send_group(e, g, True)
            if g == 1:
                send_halo(e - 1)
            if g == SECOND_AT:
                sum_second(e)

    def gather(e, table, groups, total=None):
        for g in groups:
            part = dot(table[g], receive_group(e, g))
            total = part if total is None else total + part
        return total

    def by_parameter(total):
        return [total[:, p * 128:(p + 1) * 128] for p in range(3)]

    operands[2].wait()
    ray = obs_ref[...] * LIVE[...]
    RAY[...] = ray
    pl.semaphore_wait(barrier, 30)

    @pl.loop(1, 16)
    def _(j):
        pl.semaphore_signal(entered, inc=1, device_id=b_dev(lax.rem(b_me + j, 16)), device_id_type=MESH)

    operands[3].wait()
    for t in range(TILES):
        wait_bytes(W.at[t], wsem.at[t])
        adjoint_tile(t, RAY[t:t + 1, :])
    pl.semaphore_wait(entered, 15)
    ask_first()
    send_adjoint(0, lambda: sum_first(0, total_row(ray * ray)))
    ask_second()

    def turn(t, carry):
        for k in range(BLOCKS):
            WT[t, k * 128:(k + 1) * 128, :] = W[t, k].T
        return carry

    lax.fori_loop(0, TILES, turn, 0)
    ask_third()
    back = gather(0, PICKT, range(GROUPS - 1))
    first_norm = sum_third(0)
    ray = ray / first_norm
    back = gather(0, PICKT, range(GROUPS - 1, GROUPS), back)
    model_raw = [part / first_norm for part in by_parameter(back)]

    cell = [jnp.zeros((LOCAL, 128), F32) for _ in range(3)]
    direction = model = smooth = None
    phi_bar = first_norm
    rho_bar = u_norm = rho_now = sin_term = cos_term = None
    result = [jnp.zeros((LOCAL, 128), F32) for _ in range(3)]
    most, rest = range(GROUPS - 1), range(GROUPS - 1, GROUPS)
    for i in range(ITERS):
        e = 2 * i + 1
        final = i == ITERS - 1

        for p in range(3):
            V[e - 1, p] = model_raw[p]
        send_forward(e, model_raw)
        smooth = laplace(e - 1)
        fetched = gather(e, S, most)
        v_norm = sum_third(e)
        model = [v / v_norm for v in model_raw]
        if i == 0:
            rho_bar = v_norm
            direction = model
        else:
            theta = sin_term * v_norm
            rho_bar = -cos_term * v_norm
            direction = [m - theta / rho_now * d for m, d in zip(model, direction)]
        cell_raw = [LAM * sm / v_norm - v_norm * q for sm, q in zip(smooth, cell)]
        cell_sum = total_row(sum(q * q for q in cell_raw))
        if not final:
            for p in range(3):
                V[e, p] = cell_raw[p]
            send_halo(e)
        scale = LIVE[...] / v_norm
        known = v_norm * ray
        FETCH[...] = gather(e, S, rest, fetched).astype(BF16)
        for t in range(TILES):
            TRAV[t:t + 1, :] = forward_tile(t)
        ray_raw = TRAV[...] * scale - known
        RAY[...] = ray_raw
        for t in range(0 if final else TILES):
            adjoint_tile(t, RAY[t:t + 1, :])

        ray_sum = cell_sum + total_row(ray_raw * ray_raw)

        if not final:
            send_adjoint(e + 1, lambda: sum_first(e + 1, ray_sum))
            smooth = laplace(e)
            back = gather(e + 1, PICKT, most)
            u_norm = sum_third(e + 1)
        else:
            u_norm = sum_last(ray_sum)
        rho_now = jnp.sqrt(rho_bar * rho_bar + u_norm * u_norm)
        cos_term = rho_bar / rho_now
        sin_term = u_norm / rho_now
        phi_now = cos_term * phi_bar
        phi_bar = sin_term * phi_bar
        result = [r + phi_now / rho_now * d for r, d in zip(result, direction)]
        if not final:
            ray = ray_raw / u_norm
            cell = [q / u_norm for q in cell_raw]
            known = [LAM * sm / u_norm - u_norm * m for sm, m in zip(smooth, model)]
            back = gather(e + 1, PICKT, rest, back)
            model_raw = [b / u_norm + k for b, k in zip(by_parameter(back), known)]

    for p in range(3):
        out_ref[p] = result[p]
    ratio_ref[...] = phi_bar / first_norm
    results = [
        pltpu.make_async_copy(out_ref, out_hbm, isem.at[4]),
        pltpu.make_async_copy(ratio_ref, ratio_hbm, isem.at[5]),
    ]
    for copy in results:
        copy.start()

    for e in range(EXCHANGES):
        wait_bytes(buffers(e)[0].at[pl.ds(0, DEVICES - 1)], xsend.at[e])
    for h in range(HALOS):
        for side in range(4):
            wait_bytes(HALO.at[h, side], hsend.at[h, side])
    for n in range(SUMS - 1):
        wait_bytes(AY.at[n, pl.ds(0, 15)], s1.at[n])
        wait_bytes(AZ.at[n, pl.ds(0, 15)], s2.at[n])
    wait_bytes(ALL.at[pl.ds(0, CHIPS - 1)], s2.at[SUMS - 1])
    wait_bytes(ASKED.at[0, pl.ds(0, 15)], q1.at[0])
    wait_bytes(ASKED.at[1, pl.ds(0, 15)], q2.at[0])
    for copy in results:
        copy.wait()


def shards(weights, angles, block_list, observed, ray_count):
    ang = angles.transpose(0, 2, 1, 3).reshape(TILES, 3 * BLOCKS, 128)
    anywhere = pl.BlockSpec(memory_space=pl.ANY)
    dma = pltpu.SemaphoreType.DMA
    out, ratio = pl.pallas_call(
        kernel,
        out_shape=(
            jax.ShapeDtypeStruct((3, LOCAL, 128), F32),
            jax.ShapeDtypeStruct((1, 128), F32),
        ),
        in_specs=[anywhere] * 5,
        out_specs=(anywhere, anywhere),
        scratch_shapes=[
            pltpu.VMEM((TILES, 3 * BLOCKS, 128), F32),
            pltpu.VMEM((TILES, BLOCKS), jnp.int32),
            pltpu.VMEM((TILES, 128), F32),
            pltpu.VMEM((1, 1), jnp.int32),
            pltpu.VMEM((3, LOCAL, 128), F32),
            pltpu.VMEM((1, 128), F32),
            pltpu.VMEM((TILES, BLOCKS, 128, 128), BF16),
            pltpu.VMEM((TILES, BLOCKS * 128, 128), BF16),
            pltpu.VMEM((GROUPS, ENTRIES, 2 * GROUP), BF16),
            pltpu.VMEM((SLOTS, ENTRIES), BF16),
            pltpu.VMEM((SLOTS, ENTRIES), BF16),
            pltpu.VMEM((SLOTS, LOCAL), BF16),
            pltpu.VMEM((GROUPS, LOCAL, 2 * GROUP), BF16),
            pltpu.VMEM((TILES, 128), F32),
            pltpu.VMEM((TILES, 128), F32),
            pltpu.VMEM((3, ENTRIES, 128), F32),
            pltpu.VMEM((ENTRIES, ROW), BF16),
            pltpu.VMEM((TILES, 128), F32),
            pltpu.VMEM((EXCHANGES, DEVICES, 2, ROW), BF16),
            pltpu.VMEM((EXCHANGES, DEVICES, 2, ROW), BF16),
            pltpu.VMEM((HALOS, 3, LOCAL, 128), F32),
            pltpu.VMEM((HALOS, 2, 3, 8, 128), F32),
            pltpu.VMEM((HALOS, 4, 3, 8, 128), F32),
            pltpu.VMEM((SUMS, 2, 1, 128), F32),
            pltpu.VMEM((SUMS, 16, 1, 128), F32),
            pltpu.VMEM((SUMS, 16, 1, 128), F32),
            pltpu.VMEM((CHIPS, 1, 128), F32),
            pltpu.VMEM((2, 16, 1, 128), F32),
            pltpu.VMEM((2, 16, 1, 128), F32),
            dma((TILES,)),
            dma((EXCHANGES,)),
            dma((EXCHANGES, GROUPS)),
            dma((HALOS, 4)),
            dma((HALOS, 4)),
            dma((SUMS,)),
            dma((SUMS,)),
            dma((SUMS,)),
            dma((SUMS,)),
            dma((2,)),
            dma((2,)),
            dma((6,)),
            pltpu.SemaphoreType.REGULAR,
        ],
        compiler_params=pltpu.CompilerParams(
            collective_id=0, has_side_effects=True, vmem_limit_bytes=56 * 1024 * 1024
        ),
    )(weights, ang, block_list, observed, ray_count)
    out = out.reshape(3, 8, 8, 128).transpose(1, 2, 0, 3)
    return out, ratio[0, 0]


def solution(mesh):
    placed = (
        P(("slab", "lat"), None, None, None),
        P(("slab", "lat"), None, None, None),
        P(("slab", "lat"), None),
        P(("slab", "lat"), None),
        P("slab", "lat"),
    )
    return jax.shard_map(
        shards,
        mesh=mesh,
        in_specs=placed,
        out_specs=(P("slab", "lat", None, None), P()),
        check_vma=False,
    )
```

```python
import functools

import jax
import jax.numpy as jnp
from jax import lax
from jax.experimental import pallas as pl
from jax.experimental.pallas import tpu as pltpu
from jax.sharding import PartitionSpec as P

MESH = pl.DeviceIdType.MESH
F32 = jnp.float32
BF16 = jnp.bfloat16

TILES = 12
BLOCKS = 16
ENTRIES = TILES * BLOCKS
DEVICES = 256
CHIPS = 128
N_SLAB = 8
N_LAT = 32
SLOTS = 2 * DEVICES
LOCAL = 64
ROW = 384
ITERS = 3
GROUPS = 8

Z_HALVES = ((4, 5, 3, 6), (2, 7, 1, 0))


def ring(d, n):
    return min(d, n - d)


def block_order():
    blocks = [(dx, dy, half) for dx in range(4) for dy in range(4) for half in range(2)]

    def nearness(block):
        dx, dy, half = block
        far = ring(dx, 4) + ring(dy, 4) + (2, 1)[half]
        return (-far, half, (dx * 3 + dy * 5) % 7, dx, dy)

    return sorted(blocks, key=nearness)


ORDER = block_order()
GROUP = DEVICES // GROUPS
EXCHANGES = 2 * ITERS
HALOS = EXCHANGES - 1
SUMS = EXCHANGES + 1
SECOND_AT = 5
LAM = 0.3
EPS = 1e-6


def dot(a, b):
    return lax.dot_general(a, b, (((1,), (0,)), ((), ())), preferred_element_type=F32)


def iota(shape, dim):
    return lax.broadcasted_iota(jnp.int32, shape, dim).astype(F32)


def one_hot(same):
    return jnp.where(same, 1.0, 0.0).astype(BF16)


def wait_bytes(ref, sem):
    pltpu.make_async_copy(ref, ref, sem).wait()


def block_diagonal(rows):
    place = lax.broadcasted_iota(jnp.int32, rows.shape, 0) % BLOCKS
    empty = jnp.zeros_like(rows)
    return jnp.concatenate([jnp.where(place == k, rows, empty) for k in range(BLOCKS)], axis=1)


def kernel(
    w_hbm, ang_hbm, ids_hbm, obs_hbm, cnt_hbm, out_hbm, ratio_hbm,
    ang_ref, ids_ref, obs_ref, cnt_ref, out_ref, ratio_ref,
    W, WT, S, ST, STL, PICK, PICKT, RAY, TRAV, PART, FETCH, LIVE,
    X, R, V, FACE, HALO, AX, AY, AZ, ALL, ASK, ASKED,
    wsem, xsend, xrecv, hsend, hrecv, s1, r1, s2, r2, q1, q2, isem, entered,
):
    s, l = lax.axis_index("slab"), lax.axis_index("lat")
    me = s * N_LAT + l
    y, c, z, x = lax.div(s, 2), lax.rem(s, 2), lax.div(l, 4), lax.rem(l, 4)
    a_me, b_me = z * 2 + c, y * 4 + x

    def a_dev(j):
        return (y * 2 + lax.rem(j, 2), lax.div(j, 2) * 4 + x)

    def b_dev(j):
        return (lax.div(j, 4) * 2 + c, z * 4 + lax.rem(j, 4))

    operands = [
        pltpu.make_async_copy(src, dst, isem.at[n])
        for n, (src, dst) in enumerate(
            ((ids_hbm, ids_ref), (cnt_hbm, cnt_ref), (obs_hbm, obs_ref), (ang_hbm, ang_ref))
        )
    ]

    barrier = pltpu.get_barrier_semaphore()

    @pl.loop(1, 16)
    def _(j):
        pl.semaphore_signal(barrier, inc=1, device_id=a_dev(lax.rem(a_me + j, 16)), device_id_type=MESH)
        pl.semaphore_signal(barrier, inc=1, device_id=b_dev(lax.rem(b_me + j, 16)), device_id_type=MESH)

    for copy in operands:
        copy.start()
    for t in range(TILES):
        pltpu.make_async_copy(w_hbm.at[t], W.at[t], wsem.at[t]).start()
    operands[0].wait()

    spread_k = jnp.where(
        (lax.broadcasted_iota(jnp.int32, (BLOCKS, ENTRIES), 1) & (BLOCKS - 1))
        == lax.broadcasted_iota(jnp.int32, (BLOCKS, ENTRIES), 0),
        1.0, 0.0,
    ).astype(BF16)
    own_tile = (lax.broadcasted_iota(jnp.int32, (TILES, ENTRIES), 1) >> 4) == lax.broadcasted_iota(
        jnp.int32, (TILES, ENTRIES), 0
    )

    def in_a_row(values):
        spread = dot(values.astype(F32).astype(BF16), spread_k)
        return jnp.sum(jnp.where(own_tile, spread, 0.0), axis=0, keepdims=True).astype(jnp.int32)

    ids = ids_ref[...]
    depth, cross = in_a_row(ids >> 8), in_a_row(ids & 255)
    inner = (depth & 7) * 8 + (cross & 7)
    slab_o, lat_o = depth >> 3, cross >> 3
    dx, dz = ((lat_o & 3) - x) & 3, ((lat_o >> 2) - z) & 7
    dy, dc = ((slab_o >> 1) - y) & 3, ((slab_o & 1) - c) & 1

    half = jnp.zeros_like(dz)
    place_z = jnp.zeros_like(dz)
    for h in range(2):
        for k in range(4):
            half = jnp.where(dz == Z_HALVES[h][k], h, half)
            place_z = jnp.where(dz == Z_HALVES[h][k], k, place_z)
    code = (dx * 4 + dy) * 2 + half
    place_block = jnp.zeros_like(dz)
    for n, (bx, by, bh) in enumerate(ORDER):
        place_block = jnp.where(code == (bx * 4 + by) * 2 + bh, n, place_block)
    owner = place_block * 8 + (1 - dc) * 4 + place_z
    owner_r, inner_r = owner.astype(F32), inner.astype(F32)
    square = (ENTRIES, ENTRIES)
    i0, i1 = iota(square, 0), iota(square, 1)

    def column(row):
        return jnp.sum(jnp.where(i0 == i1, row, 0.0), axis=1, keepdims=True)

    owner_c, inner_c = column(owner_r), column(inner_r)
    same = jnp.where(owner_r == owner_c, 1.0, 0.0)
    slot_c = 2.0 * owner_c + jnp.sum(jnp.where(i1 < i0, same, 0.0), axis=1, keepdims=True)
    slot_r = 2.0 * owner_r + jnp.sum(jnp.where(i0 < i1, same, 0.0), axis=0, keepdims=True)
    alone = jnp.sum(same, axis=0, keepdims=True) == 1.0
    spare_r = jnp.where(alone, slot_r + 1.0, -1.0)
    for g in range(GROUPS):
        S[g] = one_hot(iota((ENTRIES, 2 * GROUP), 1) + float(2 * GROUP * g) == slot_c)
    st = one_hot(iota((SLOTS, ENTRIES), 0) == slot_r)
    stl = one_hot(iota((SLOTS, ENTRIES), 0) == spare_r)
    ST[...] = st
    STL[...] = stl

    rank_r = slot_r - 2.0 * owner_r
    a_r = ((lat_o >> 2) * 2 + (slab_o & 1)).astype(F32)
    lane_r = 2.0 * ((slab_o >> 1) * 4 + (lat_o & 3)).astype(F32) + rank_r
    lane_c = column(lane_r)
    spare_c = column(jnp.where(alone, lane_r + 1.0, -1.0))
    lanes = iota((ENTRIES, 128), 1)
    asked = dot(
        jnp.where(iota((16, ENTRIES), 0) == a_r, inner_r + 1.0, 0.0).astype(BF16),
        one_hot(lanes == lane_c) + one_hot(lanes == spare_c),
    )

    def ask_first():
        for i in range(16):
            ASK[0, i] = asked[i:i + 1]
        ASKED[0, a_me] = ASK[0, a_me]

        @pl.loop(1, 16)
        def _(j):
            d = lax.rem(a_me + j, 16)
            pltpu.make_async_remote_copy(
                ASK.at[0, d], ASKED.at[0, a_me], q1.at[0], q1.at[1], device_id=a_dev(d), device_id_type=MESH
            ).start()

    def ask_second():
        wait_bytes(ASKED.at[0, pl.ds(0, 15)], q1.at[1])
        rows = jnp.concatenate([ASKED[0, i] for i in range(16)], axis=0).astype(BF16)
        turned = None
        for r in range(2):
            mine = one_hot(iota((16, 128), 1) == 2.0 * iota((16, 128), 0) + float(r))
            part = lax.dot_general(mine, rows, (((1,), (1,)), ((), ())), preferred_element_type=F32)
            part = dot(part.astype(BF16), mine)
            turned = part if turned is None else turned + part
        for i in range(16):
            ASK[1, i] = turned[i:i + 1]
        ASKED[1, b_me] = ASK[1, b_me]

        @pl.loop(1, 16)
        def _(j):
            d = lax.rem(b_me + j, 16)
            pltpu.make_async_remote_copy(
                ASK.at[1, d], ASKED.at[1, b_me], q2.at[0], q2.at[1], device_id=b_dev(d), device_id_type=MESH
            ).start()

    def ask_third():
        slot = lax.broadcasted_iota(jnp.int32, (1, SLOTS), 1)
        block, core, k = slot >> 4, (slot >> 3) & 1, (slot >> 1) & 3
        from_x, from_y, half = jnp.zeros_like(slot), jnp.zeros_like(slot), jnp.zeros_like(slot)
        for n, (bx, by, bh) in enumerate(ORDER):
            here = block == n
            from_x = jnp.where(here, (x - bx) & 3, from_x)
            from_y = jnp.where(here, (y - by) & 3, from_y)
            half = jnp.where(here, bh, half)
        from_z = jnp.zeros_like(slot)
        for h in range(2):
            for n in range(4):
                from_z = jnp.where(half * 4 + k == h * 4 + n, (z - Z_HALVES[h][n]) & 7, from_z)
        from_c = (c + 1 - core) & 1
        a_s = (from_z * 2 + from_c).astype(F32)
        b_s = (from_y * 4 + from_x).astype(F32)
        lane_s = 2.0 * a_s + (slot & 1).astype(F32)
        lane_table = one_hot(iota((128, SLOTS), 0) == lane_s)
        wait_bytes(ASKED.at[1, pl.ds(0, 15)], q2.at[1])
        rows = jnp.concatenate([ASKED[1, i] for i in range(16)], axis=0).astype(BF16)
        found = jnp.where(iota((16, SLOTS), 0) == b_s, dot(rows, lane_table), 0.0)
        inner_s = jnp.sum(found, axis=0, keepdims=True) - 1.0
        picked = jnp.where(iota((LOCAL, SLOTS), 0) == inner_s, 1.0, 0.0)
        PICK[...] = picked.T.astype(BF16)
        for g in range(GROUPS):
            PICKT[g] = PICK[pl.ds(g * 2 * GROUP, 2 * GROUP), :].T


    at = iota((TILES, 128), 0) * 128.0 + iota((TILES, 128), 1)
    operands[1].wait()
    LIVE[...] = jnp.where(at < cnt_ref[...].astype(F32), 1.0, 0.0)

    def total_row(values):
        return jnp.sum(values, axis=0, keepdims=True)

    def sum_first(n, row):
        AX[n, 0] = row
        AY[n, a_me] = row

        @pl.loop(1, 16)
        def _(j):
            pltpu.make_async_remote_copy(
                AX.at[n, 0], AY.at[n, a_me], s1.at[n], r1.at[n],
                device_id=a_dev(lax.rem(a_me + j, 16)), device_id_type=MESH,
            ).start()

    def sum_second(n):
        wait_bytes(AY.at[n, pl.ds(0, 15)], r1.at[n])
        row = jnp.sum(AY[n], axis=0)
        AX[n, 1] = row
        AZ[n, b_me] = row

        @pl.loop(1, 16)
        def _(j):
            pltpu.make_async_remote_copy(
                AX.at[n, 1], AZ.at[n, b_me], s2.at[n], r2.at[n],
                device_id=b_dev(lax.rem(b_me + j, 16)), device_id_type=MESH,
            ).start()

    def sum_third(n):
        wait_bytes(AZ.at[n, pl.ds(0, 15)], r2.at[n])
        total = jnp.sum(jnp.sum(AZ[n], axis=0), axis=1, keepdims=True)
        return jnp.sqrt(jnp.broadcast_to(total, (1, 128)) + EPS)

    def sum_last(row):
        n = SUMS - 1
        AX[n, 0] = row
        pair = pltpu.make_async_remote_copy(
            AX.at[n, 0], AY.at[n, 0], s1.at[n], r1.at[n], device_id=(y * 2 + 1 - c, l), device_id_type=MESH
        )
        pair.start()
        pair.wait()
        row = row + AY[n, 0]
        AX[n, 1] = row
        ALL[CHIPS - 1] = row

        def one(j, to_y, to_x, dz):
            pltpu.make_async_remote_copy(
                AX.at[n, 1], ALL.at[j], s2.at[n], r2.at[n],
                device_id=(to_y * 2 + c, lax.rem(z + dz, 8) * 4 + to_x), device_id_type=MESH,
            ).start()

        def offset(i):
            far = 3 - i
            return lax.rem(lax.div(far * (far + 1), 2), 4)

        steps = Z_HALVES[0] + Z_HALVES[1]

        @pl.loop(0, 15)
        def _(q):
            to_x = lax.rem(x + offset(lax.div(q, 4)), 4)
            to_y = lax.rem(y + offset(lax.rem(q, 4)), 4)
            for k in range(8):
                one(q * 8 + k, to_y, to_x, steps[k])

        for k in range(7):
            one(120 + k, y, x, steps[k])
        wait_bytes(ALL.at[pl.ds(0, CHIPS - 1)], r2.at[n])
        total = jnp.sum(jnp.sum(ALL[...], axis=0), axis=1, keepdims=True)
        return jnp.sqrt(jnp.broadcast_to(total, (1, 128)) + EPS)

    def buffers(e):
        return X.at[e], R.at[e]

    def send_group(e, g, forward):
        src, dst = buffers(e)
        blocks = ORDER[g * 4:(g + 1) * 4]

        def of_block(b, values):
            value = values[0]
            for n in range(1, 4):
                value = jnp.where(b == n, values[n], value)
            return value

        def place(at, d, n):
            return lax.rem(at + n - d, n) if forward else lax.rem(at + d, n)

        def one(i, k, to_z, to_x, to_slab):
            j = g * GROUP + i * 4 + k
            pltpu.make_async_remote_copy(
                src.at[j], dst.at[j], xsend.at[e], xrecv.at[e, g],
                device_id=(to_slab, to_z * 4 + to_x), device_id_type=MESH,
            ).start()

        @pl.loop(0, 7 if g == GROUPS - 1 else 8)
        def _(i):
            b = lax.div(i, 2)
            to_x = place(x, of_block(b, [n[0] for n in blocks]), 4)
            to_y = place(y, of_block(b, [n[1] for n in blocks]), 4)
            to_c = lax.rem(c + 1 - lax.rem(i, 2), 2)
            for k in range(4):
                dz = of_block(b, [Z_HALVES[n[2]][k] for n in blocks])
                one(i, k, place(z, dz, 8), to_x, to_y * 2 + to_c)

        if g == GROUPS - 1:
            for k in range(3):
                one(7, k, place(z, Z_HALVES[1][k], 8), x, s)
            pltpu.make_async_copy(src.at[DEVICES - 1], dst.at[DEVICES - 1], xrecv.at[e, g]).start()

    def receive_group(e, g):
        dst = buffers(e)[1].at[pl.ds(g * GROUP, GROUP)]
        wait_bytes(dst, xrecv.at[e, g])
        return dst[...].reshape(2 * GROUP, dst.shape[-1])

    def send_halo(h):
        for p in range(3):
            v = V[h, p]
            FACE[h, 0, p] = jnp.concatenate([v[8 * i:8 * i + 1] for i in range(8)], axis=0)
            FACE[h, 1, p] = jnp.concatenate([v[8 * i + 7:8 * i + 8] for i in range(8)], axis=0)
        before, after = lax.rem(s + N_SLAB - 1, N_SLAB), lax.rem(s + 1, N_SLAB)
        left, right = lax.rem(l + N_LAT - 1, N_LAT), lax.rem(l + 1, N_LAT)
        moves = (
            (V.at[h, :, pl.ds(56, 8)], 0, (after, l)),
            (V.at[h, :, pl.ds(0, 8)], 1, (before, l)),
            (FACE.at[h, 1], 2, (s, right)),
            (FACE.at[h, 0], 3, (s, left)),
        )
        for src, side, device in moves:
            pltpu.make_async_remote_copy(
                src, HALO.at[h, side], hsend.at[h, side], hrecv.at[h, side],
                device_id=device, device_id_type=MESH,
            ).start()

    def laplace(h):
        for side in range(4):
            wait_bytes(HALO.at[h, side], hrecv.at[h, side])
        row = lax.broadcasted_iota(jnp.int32, (LOCAL, 128), 0) % 8
        lane = lax.broadcasted_iota(jnp.int32, (LOCAL, 128), 1)

        def spread(face):
            return jnp.concatenate([jnp.broadcast_to(face[i:i + 1], (8, 128)) for i in range(8)], axis=0)

        result = []
        for p in range(3):
            v = V[h, p]
            low = jnp.where(s > 0, HALO[h, 0, p], 0.0)
            high = jnp.where(s < N_SLAB - 1, HALO[h, 1, p], 0.0)
            left = jnp.where(l > 0, HALO[h, 2, p], 0.0)
            right = jnp.where(l < N_LAT - 1, HALO[h, 3, p], 0.0)
            beside = jnp.concatenate([low, v[:56]], axis=0) + jnp.concatenate([v[8:], high], axis=0)
            beside = beside + jnp.where(row == 0, spread(left), pltpu.roll(v, 1, 0))
            beside = beside + jnp.where(row == 7, spread(right), pltpu.roll(v, LOCAL - 1, 0))
            beside = beside + jnp.where(lane == 0, 0.0, pltpu.roll(v, 1, 1))
            beside = beside + jnp.where(lane == 127, 0.0, pltpu.roll(v, 127, 1))
            result.append(6.0 * v - beside)
        return result

    def forward_tile(t):
        rows = jnp.concatenate(
            [FETCH[t * BLOCKS:(t + 1) * BLOCKS, p * 128:(p + 1) * 128] for p in range(3)], axis=0
        )
        return total_row(dot(block_diagonal(rows), WT[t]) * ang_ref[t])

    def adjoint_tile(t, ray_row):
        weighted = ang_ref[t] * ray_row
        high = weighted.astype(BF16)
        low = (weighted - high.astype(F32)).astype(BF16)
        rows = block_diagonal(jnp.concatenate([high, low], axis=0))
        out = dot(rows, W[t].reshape(BLOCKS * 128, 128))
        out = out[:48] + out[48:]
        for p in range(3):
            PART[p, t * BLOCKS:(t + 1) * BLOCKS, :] = out[p * BLOCKS:(p + 1) * BLOCKS]

    def send_adjoint(e, beside):
        high = [PART[p].astype(BF16) for p in range(3)]
        low = [(PART[p] - high[p].astype(F32)).astype(BF16) for p in range(3)]
        high, low = jnp.concatenate(high, axis=1), jnp.concatenate(low, axis=1)
        for g in range(GROUPS):
            at = pl.ds(g * 2 * GROUP, 2 * GROUP)
            rows = (dot(ST[at, :], high) + dot(STL[at, :], low)).astype(BF16)
            src = buffers(e)[0]
            src[pl.ds(g * GROUP, GROUP)] = rows.reshape(GROUP, 2, rows.shape[-1])
            if g == 0:
                beside()
            send_group(e, g, False)
            if g == SECOND_AT:
                sum_second(e)

    def send_forward(e, values):
        model = jnp.concatenate(values, axis=1).astype(BF16)
        for g in range(GROUPS):
            rows = dot(PICK[pl.ds(g * 2 * GROUP, 2 * GROUP), :], model).astype(BF16)
            buffers(e)[0][pl.ds(g * GROUP, GROUP)] = rows.reshape(GROUP, 2, ROW)
            if g == 0:
                sum_first(e, total_row(sum(v * v for v in values)))
            send_group(e, g, True)
            if g == 1:
                send_halo(e - 1)
            if g == SECOND_AT:
                sum_second(e)

    def gather(e, table, groups, total=None):
        for g in groups:
            part = dot(table[g], receive_group(e, g))
            total = part if total is None else total + part
        return total

    def by_parameter(total):
        return [total[:, p * 128:(p + 1) * 128] for p in range(3)]

    operands[2].wait()
    ray = obs_ref[...] * LIVE[...]
    RAY[...] = ray
    pl.semaphore_wait(barrier, 30)

    @pl.loop(1, 16)
    def _(j):
        pl.semaphore_signal(entered, inc=1, device_id=b_dev(lax.rem(b_me + j, 16)), device_id_type=MESH)

    operands[3].wait()
    for t in range(TILES):
        wait_bytes(W.at[t], wsem.at[t])
        adjoint_tile(t, RAY[t:t + 1, :])
    pl.semaphore_wait(entered, 15)
    ask_first()
    send_adjoint(0, lambda: sum_first(0, total_row(ray * ray)))
    ask_second()

    def turn(t, carry):
        for k in range(BLOCKS):
            WT[t, k * 128:(k + 1) * 128, :] = W[t, k].T
        return carry

    lax.fori_loop(0, TILES, turn, 0)
    ask_third()
    back = gather(0, PICKT, range(GROUPS - 1))
    first_norm = sum_third(0)
    ray = ray / first_norm
    back = gather(0, PICKT, range(GROUPS - 1, GROUPS), back)
    model_raw = [part / first_norm for part in by_parameter(back)]

    cell = [jnp.zeros((LOCAL, 128), F32) for _ in range(3)]
    direction = model = smooth = None
    phi_bar = first_norm
    rho_bar = u_norm = rho_now = sin_term = cos_term = None
    result = [jnp.zeros((LOCAL, 128), F32) for _ in range(3)]
    most, rest = range(GROUPS - 1), range(GROUPS - 1, GROUPS)
    for i in range(ITERS):
        e = 2 * i + 1
        final = i == ITERS - 1

        for p in range(3):
            V[e - 1, p] = model_raw[p]
        send_forward(e, model_raw)
        smooth = laplace(e - 1)
        fetched = gather(e, S, most)
        v_norm = sum_third(e)
        model = [v / v_norm for v in model_raw]
        if i == 0:
            rho_bar = v_norm
            direction = model
        else:
            theta = sin_term * v_norm
            rho_bar = -cos_term * v_norm
            direction = [m - theta / rho_now * d for m, d in zip(model, direction)]
        cell_raw = [LAM * sm / v_norm - v_norm * q for sm, q in zip(smooth, cell)]
        cell_sum = total_row(sum(q * q for q in cell_raw))
        if not final:
            for p in range(3):
                V[e, p] = cell_raw[p]
            send_halo(e)
        scale = LIVE[...] / v_norm
        known = v_norm * ray
        FETCH[...] = gather(e, S, rest, fetched).astype(BF16)
        for t in range(TILES):
            TRAV[t:t + 1, :] = forward_tile(t)
        ray_raw = TRAV[...] * scale - known
        RAY[...] = ray_raw
        for t in range(0 if final else TILES):
            adjoint_tile(t, RAY[t:t + 1, :])

        ray_sum = cell_sum + total_row(ray_raw * ray_raw)

        if not final:
            send_adjoint(e + 1, lambda: sum_first(e + 1, ray_sum))
            smooth = laplace(e)
            back = gather(e + 1, PICKT, most)
            u_norm = sum_third(e + 1)
        else:
            u_norm = sum_last(ray_sum)
        rho_now = jnp.sqrt(rho_bar * rho_bar + u_norm * u_norm)
        cos_term = rho_bar / rho_now
        sin_term = u_norm / rho_now
        phi_now = cos_term * phi_bar
        phi_bar = sin_term * phi_bar
        result = [r + phi_now / rho_now * d for r, d in zip(result, direction)]
        if not final:
            ray = ray_raw / u_norm
            cell = [q / u_norm for q in cell_raw]
            known = [LAM * sm / u_norm - u_norm * m for sm, m in zip(smooth, model)]
            back = gather(e + 1, PICKT, rest, back)
            model_raw = [b / u_norm + k for b, k in zip(by_parameter(back), known)]

    for p in range(3):
        out_ref[p] = result[p]
    ratio_ref[...] = phi_bar / first_norm
    results = [
        pltpu.make_async_copy(out_ref, out_hbm, isem.at[4]),
        pltpu.make_async_copy(ratio_ref, ratio_hbm, isem.at[5]),
    ]
    for copy in results:
        copy.start()

    for e in range(EXCHANGES):
        wait_bytes(buffers(e)[0].at[pl.ds(0, DEVICES - 1)], xsend.at[e])
    for h in range(HALOS):
        for side in range(4):
            wait_bytes(HALO.at[h, side], hsend.at[h, side])
    for n in range(SUMS - 1):
        wait_bytes(AY.at[n, pl.ds(0, 15)], s1.at[n])
        wait_bytes(AZ.at[n, pl.ds(0, 15)], s2.at[n])
    wait_bytes(ALL.at[pl.ds(0, CHIPS - 1)], s2.at[SUMS - 1])
    wait_bytes(ASKED.at[0, pl.ds(0, 15)], q1.at[0])
    wait_bytes(ASKED.at[1, pl.ds(0, 15)], q2.at[0])
    for copy in results:
        copy.wait()


def shards(weights, angles, block_list, observed, ray_count):
    ang = angles.transpose(0, 2, 1, 3).reshape(TILES, 3 * BLOCKS, 128)
    anywhere = pl.BlockSpec(memory_space=pl.ANY)
    dma = pltpu.SemaphoreType.DMA
    out, ratio = pl.pallas_call(
        kernel,
        out_shape=(
            jax.ShapeDtypeStruct((3, LOCAL, 128), F32),
            jax.ShapeDtypeStruct((1, 128), F32),
        ),
        in_specs=[anywhere] * 5,
        out_specs=(anywhere, anywhere),
        scratch_shapes=[
            pltpu.VMEM((TILES, 3 * BLOCKS, 128), F32),
            pltpu.VMEM((TILES, BLOCKS), jnp.int32),
            pltpu.VMEM((TILES, 128), F32),
            pltpu.VMEM((1, 1), jnp.int32),
            pltpu.VMEM((3, LOCAL, 128), F32),
            pltpu.VMEM((1, 128), F32),
            pltpu.VMEM((TILES, BLOCKS, 128, 128), BF16),
            pltpu.VMEM((TILES, BLOCKS * 128, 128), BF16),
            pltpu.VMEM((GROUPS, ENTRIES, 2 * GROUP), BF16),
            pltpu.VMEM((SLOTS, ENTRIES), BF16),
            pltpu.VMEM((SLOTS, ENTRIES), BF16),
            pltpu.VMEM((SLOTS, LOCAL), BF16),
            pltpu.VMEM((GROUPS, LOCAL, 2 * GROUP), BF16),
            pltpu.VMEM((TILES, 128), F32),
            pltpu.VMEM((TILES, 128), F32),
            pltpu.VMEM((3, ENTRIES, 128), F32),
            pltpu.VMEM((ENTRIES, ROW), BF16),
            pltpu.VMEM((TILES, 128), F32),
            pltpu.VMEM((EXCHANGES, DEVICES, 2, ROW), BF16),
            pltpu.VMEM((EXCHANGES, DEVICES, 2, ROW), BF16),
            pltpu.VMEM((HALOS, 3, LOCAL, 128), F32),
            pltpu.VMEM((HALOS, 2, 3, 8, 128), F32),
            pltpu.VMEM((HALOS, 4, 3, 8, 128), F32),
            pltpu.VMEM((SUMS, 2, 1, 128), F32),
            pltpu.VMEM((SUMS, 16, 1, 128), F32),
            pltpu.VMEM((SUMS, 16, 1, 128), F32),
            pltpu.VMEM((CHIPS, 1, 128), F32),
            pltpu.VMEM((2, 16, 1, 128), F32),
            pltpu.VMEM((2, 16, 1, 128), F32),
            dma((TILES,)),
            dma((EXCHANGES,)),
            dma((EXCHANGES, GROUPS)),
            dma((HALOS, 4)),
            dma((HALOS, 4)),
            dma((SUMS,)),
            dma((SUMS,)),
            dma((SUMS,)),
            dma((SUMS,)),
            dma((2,)),
            dma((2,)),
            dma((6,)),
            pltpu.SemaphoreType.REGULAR,
        ],
        compiler_params=pltpu.CompilerParams(
            collective_id=0, has_side_effects=True, vmem_limit_bytes=56 * 1024 * 1024
        ),
    )(weights, ang, block_list, observed, ray_count)
    out = out.reshape(3, 8, 8, 128).transpose(1, 2, 0, 3)
    return out, ratio[0, 0]


def solution(mesh):
    placed = (
        P(("slab", "lat"), None, None, None),
        P(("slab", "lat"), None, None, None),
        P(("slab", "lat"), None),
        P(("slab", "lat"), None),
        P("slab", "lat"),
    )
    return jax.shard_map(
        shards,
        mesh=mesh,
        in_specs=placed,
        out_specs=(P("slab", "lat", None, None), P()),
        check_vma=False,
    )
```
